128 devices in a mesh: dp: 4 (over z_hi, core), fsdp: 32 (over z_lo, y, x).
Axes of the slice: x: 4, y: 4, z: 4 (z_hi: 2, z_lo: 2; z = z_hi * 2 + z_lo), core: 2. Of those that a mesh axis runs over, the one named last changes fastest.
Arguments:
- grads: bfloat16 [4, 8192, 16384], P('dp', None, 'fsdp'), may hold values from -6 to 6
- basis: bfloat16 [8192, 1024], P(('dp', 'fsdp')), may hold values from -0.1875 to 0.1875
- first_moment: float32 [1024, 16384], P('dp', 'fsdp'), may hold values from -3 to 3
- second_moment: float32 [1024, 16384], P('dp', 'fsdp'), may hold values from 0.5 to 4
Outputs:
- update: bfloat16 [8192, 16384], P(None, 'fsdp')
- new_first: float32 [1024, 16384], P('dp', 'fsdp')
- new_second: float32 [1024, 16384], P('dp', 'fsdp')
The draws below stay inside these ranges and needn't reach their ends.
All inputs are finite; a program needn't handle non-finite values.
Results may differ from the reference program's by a relative error of at most 0.005.
Values may be sent and summed in bfloat16 or wider, within the bound.
No kernel may reach another device: no remote copies, remote signals or barrier semaphores. Data moves between devices by JAX's collectives and lax.ppermute only.
A program may use at most 128 MiB of HBM per device.

```python
import math
import jax
import jax.numpy as jnp

D = 8192
FFW = 16384
R = 1024
N_DP = 4


def block_scale(stream_key, extent, cuts, low, top_value):
    def one(dim, blocks):
        heights = jax.random.uniform(jax.random.fold_in(jax.random.fold_in(stream_key, 6), dim), (blocks,), jnp.float32, low / len(cuts), top_value / len(cuts))
        return jnp.repeat(jnp.exp(heights), extent[dim] // blocks).reshape((-1,) + (1,) * (len(extent) - dim - 1))

    level = one(*cuts[0])
    for cut in cuts[1:]:
        level = level * one(*cut)
    return level


def scatter_about(key, dims, deviation, bound, pieces=(), kind=jnp.bfloat16):
    array = jax.random.normal(key, dims, jnp.float32) * deviation
    if len(pieces) > 0:
        array = block_scale(key, dims, pieces, -0.22, 0.18) * array
    return jnp.clip(array, min=-bound, max=bound).astype(kind)


def setup_inputs(seed: int = 0) -> dict:
    key_of = jax.random.split(jax.random.key(seed), 5)
    grads = scatter_about(key_of[0], (N_DP, D, FFW), 1.0, 6.0, ((0, 4), (2, 32)))
    basis = scatter_about(key_of[1], (D, R), R ** -0.5, 0.1875, ((0, 128),))
    first_moment = scatter_about(key_of[2], (R, FFW), 0.3, 3.0, ((0, 4), (1, 32)), jnp.float32)
    second_moment = jnp.clip(jnp.exp(math.log(4.0) - 2.0794415 * jax.random.uniform(key_of[3], (R, FFW), jnp.float32) ** block_scale(key_of[3], (R, FFW), ((0, 4), (1, 32)), -0.2, 0.2)), 0.5, 4.0)
    return {"grads": grads, "basis": basis, "first_moment": first_moment, "second_moment": second_moment}


first_fix = 1.0 - math.exp(1000.0 * math.log(0.9))
second_fix = 1.0 - math.exp(1000.0 * math.log(0.999))

def reference(grads, basis, first_moment, second_moment):
    basis_t = basis.T
    total = jnp.zeros((R, FFW), jnp.float32)
    for group in range(N_DP):
        total = total + jnp.dot(basis_t, grads[group], preferred_element_type=jnp.float32)
    projected = total * (1.0 / N_DP)
    new_first = 0.9 * first_moment + 0.1 * projected
    new_second = 0.999 * second_moment + 0.001 * projected * projected
    direction = (new_first / first_fix / (jnp.sqrt(new_second / second_fix) + 1e-08)).astype(jnp.bfloat16)
    update = jnp.dot(basis, direction, preferred_element_type=jnp.float32).astype(jnp.bfloat16)
    return (update, new_first, new_second)
```

```python
import math

import jax
import jax.numpy as jnp
from jax import lax
from jax.experimental import pallas as pl
from jax.experimental.pallas import tpu as pltpu
from jax.sharding import PartitionSpec as P

first_fix = 1.0 - math.exp(1000.0 * math.log(0.9))
second_fix = 1.0 - math.exp(1000.0 * math.log(0.999))

BOTH = ("dp", "fsdp")
STREAMS = ((0, 384, "zyx"), (384, 768, "yxz"), (768, 1024, "xzy"))
ORDER = ((0, 1, 3, 2), (0, 3, 1, 2))


def pairs(partner):
    out = []
    for c in range(2):
        for z in range(4):
            for y in range(4):
                for x in range(4):
                    out.append((linear(c, z, y, x), linear(*partner(c, z, y, x))))
    return out


def linear(c, z, y, x):
    return (((z // 2) * 2 + c) * 2 + z % 2) * 16 + y * 4 + x


def exchange(value, axis, step):
    def partner(c, z, y, x):
        t = ORDER[c][1] if step == 0 else ORDER[1 - c][1]
        return c, z ^ t if axis == "z" else z, y ^ t if axis == "y" else y, x ^ t if axis == "x" else x

    return lax.ppermute(value, BOTH, pairs(partner))


def swap_core(value):
    return lax.ppermute(value, BOTH, pairs(lambda c, z, y, x: (1 - c, z, y, x)))


def swap_far(value):
    return lax.ppermute(value, BOTH, pairs(lambda c, z, y, x: (c, z ^ 2, y, x)))


def gather(shard, order):
    held = shard[None, None, None]
    for axis in order:
        for step in range(2):
            held = jnp.concatenate([held, exchange(held, axis, step)], axis="zyx".index(axis))
    return held


def place(core, block):
    return jnp.where(core == 0, ORDER[0][block], ORDER[1][block])


def row_of(core, of_core, z, y, x, index):
    a, b, c = index // 16, (index // 4) % 4, index % 4

    def off(p):
        one = jnp.where(of_core == 0, 1, 3)
        return jnp.where(p == 0, 0, jnp.where(p == 1, one, jnp.where(p == 2, 4 - one, 2)))

    zz, yy, xx = z ^ off(a), y ^ off(b), x ^ off(c)
    return (((zz // 2) * 2 + of_core) * 2 + zz % 2) * 1024 + yy * 256 + xx * 64


def split_kernel(where, grads, own, other, sems):
    core, z, y, x = where[0], where[1], where[2], where[3]

    def body(i, carry):
        for k, (out, of_core) in enumerate(((own, core), (other, 1 - core))):
            row = pl.multiple_of(row_of(core, of_core, z, y, x, i), 64)
            pltpu.make_async_copy(
                grads.at[pl.ds(row, 64)], out.at[pl.ds(pl.multiple_of(i * 64, 64), 64)], sems.at[k]
            ).start()
        return carry

    lax.fori_loop(0, 64, body, 0)
    pltpu.make_async_copy(own, own, sems.at[0]).wait()
    pltpu.make_async_copy(other, other, sems.at[1]).wait()


def split_grads(where, grads):
    half = jax.ShapeDtypeStruct((grads.shape[0] // 2, grads.shape[1]), grads.dtype)
    return pl.pallas_call(
        split_kernel,
        out_shape=(half, half),
        grid_spec=pltpu.PrefetchScalarGridSpec(
            num_scalar_prefetch=1,
            grid=(),
            in_specs=[pl.BlockSpec(memory_space=pl.ANY)],
            out_specs=[pl.BlockSpec(memory_space=pl.ANY)] * 2,
            scratch_shapes=[pltpu.SemaphoreType.DMA((2,))],
        ),
        name="split_grads",
    )(where, grads)


TILE = 512


def update_kernel(where, own, other, direction, out, result, sems):
    core, z, y, x = where[0], where[1], where[2], where[3]
    step = pl.program_id(0)
    half = pl.num_programs(0) // 2
    slot = step % 2

    def drain(k):
        pltpu.make_async_copy(result.at[k], result.at[k], sems.at[k]).wait()

    @pl.when(step >= 2)
    def _():
        drain(slot)

    def go(basis, of_core, base):
        result[slot] = jnp.dot(
            basis[...], direction[...], preferred_element_type=jnp.float32
        ).astype(jnp.bfloat16)
        for j in range(TILE // 64):
            row = pl.multiple_of(row_of(core, of_core, z, y, x, base * (TILE // 64) + j), 64)
            pltpu.make_async_copy(
                result.at[slot, pl.ds(j * 64, 64)], out.at[pl.ds(row, 64)], sems.at[slot]
            ).start()

    @pl.when(step < half)
    def _():
        go(own, core, step)

    @pl.when(step >= half)
    def _():
        go(other, 1 - core, step - half)

    @pl.when(step == 2 * half - 1)
    def _():
        drain(1 - slot)
        drain(slot)


def back_project(where, own, other, direction):
    rows, rank = own.shape
    columns = direction.shape[1]
    half = rows // TILE
    return pl.pallas_call(
        update_kernel,
        out_shape=jax.ShapeDtypeStruct((2 * rows, columns), jnp.bfloat16),
        grid_spec=pltpu.PrefetchScalarGridSpec(
            num_scalar_prefetch=1,
            grid=(2 * half,),
            in_specs=[
                pl.BlockSpec((TILE, rank), lambda i, w: (jnp.minimum(i, half - 1), 0)),
                pl.BlockSpec((TILE, rank), lambda i, w: (jnp.maximum(i - half, 0), 0)),
                pl.BlockSpec((rank, columns), lambda i, w: (0, 0)),
            ],
            out_specs=pl.BlockSpec(memory_space=pl.ANY),
            scratch_shapes=[
                pltpu.VMEM((2, TILE, columns), jnp.bfloat16),
                pltpu.SemaphoreType.DMA((2,)),
            ],
        ),
        compiler_params=pltpu.CompilerParams(vmem_limit_bytes=32 * 1024 * 1024),
        name="back_project",
    )(where, own, other, direction)


def local(grads, basis, first_moment, second_moment):
    dp, fsdp = lax.axis_index("dp"), lax.axis_index("fsdp")
    far, core = dp // 2, dp % 2
    z, y, x = far * 2 + fsdp // 16, (fsdp // 4) % 4, fsdp % 4
    where = jnp.stack([core, z, y, x]).astype(jnp.int32)

    mine, theirs = split_grads(where, grads[0])
    summed_grads = (mine.astype(jnp.float32) + swap_core(theirs).astype(jnp.float32)).astype(jnp.bfloat16)

    chunks = [gather(basis[:, low:high], order).reshape(-1, high - low) for low, high, order in STREAMS]
    partial = jnp.concatenate(
        [
            lax.dot_general(chunk, summed_grads, (((0,), (0,)), ((), ())), preferred_element_type=jnp.float32)
            for chunk in chunks
        ]
    )
    own_basis = jnp.concatenate(chunks, axis=1)
    other_basis = swap_core(own_basis)

    share, columns = first_moment.shape
    partial = partial.reshape(2, 2, share, columns)
    kept = lax.dynamic_index_in_dim(partial, core, 1, keepdims=False)
    sent = lax.dynamic_index_in_dim(partial, 1 - core, 1, keepdims=False)
    chip = kept + swap_core(sent)
    kept = lax.dynamic_index_in_dim(chip, far, 0, keepdims=False)
    sent = lax.dynamic_index_in_dim(chip, 1 - far, 0, keepdims=False)
    total = kept + swap_far(sent.astype(jnp.bfloat16)).astype(jnp.float32)

    projected = total * (1.0 / 4)
    new_first = 0.9 * first_moment + 0.1 * projected
    new_second = 0.999 * second_moment + 0.001 * projected * projected
    direction = (new_first / first_fix / (jnp.sqrt(new_second / second_fix) + 1e-08)).astype(jnp.bfloat16)

    received = swap_far(direction)
    pair = jnp.stack([jnp.where(far == 0, direction, received), jnp.where(far == 0, received, direction)])
    received = swap_core(pair)
    whole = jnp.stack([jnp.where(core == 0, pair, received), jnp.where(core == 0, received, pair)], axis=1)
    update = back_project(where, own_basis, other_basis, whole.reshape(4 * share, columns))
    return (update, new_first, new_second)


def solution(mesh):
    return jax.shard_map(
        local,
        mesh=mesh,
        in_specs=(P("dp", None, "fsdp"), P(("dp", "fsdp"), None), P("dp", "fsdp"), P("dp", "fsdp")),
        out_specs=(P(None, "fsdp"), P("dp", "fsdp"), P("dp", "fsdp")),
        check_vma=False,
    )
```

```python
import functools
import math

import jax
import jax.numpy as jnp
from jax import lax
from jax.experimental import pallas as pl
from jax.experimental.pallas import tpu as pltpu
from jax.sharding import PartitionSpec as P

first_fix = 1.0 - math.exp(1000.0 * math.log(0.9))
second_fix = 1.0 - math.exp(1000.0 * math.log(0.999))

BOTH = ("dp", "fsdp")
ORDER = ((0, 1, 3, 2), (0, 3, 1, 2))
STREAMS = ((0, 384, "x"), (384, 768, "y"), (768, 1024, "z"))
MIB = 1024 * 1024


def linear(c, z, y, x):
    return (((z // 2) * 2 + c) * 2 + z % 2) * 16 + y * 4 + x


def pairs(partner):
    return [
        (linear(c, z, y, x), linear(*partner(c, z, y, x)))
        for c in range(2)
        for z in range(4)
        for y in range(4)
        for x in range(4)
    ]


def exchange(value, axis, step):
    def partner(c, z, y, x):
        t = ORDER[c][1] if step == 0 else ORDER[1 - c][1]
        return c, z ^ t if axis == "z" else z, y ^ t if axis == "y" else y, x ^ t if axis == "x" else x

    return lax.ppermute(value, BOTH, pairs(partner))


def swap_core(value):
    return lax.ppermute(value, BOTH, pairs(lambda c, z, y, x: (1 - c, z, y, x)))


def swap_far(value):
    return lax.ppermute(value, BOTH, pairs(lambda c, z, y, x: (c, z ^ 2, y, x)))


def grow(held, axis, step):
    return jnp.concatenate([held, exchange(held, axis, step)], axis="zyx".index(axis))


def together(*values):
    return lax.optimization_barrier(values)


def offset(of_core, position):
    one = jnp.where(of_core == 0, 1, 3)
    return jnp.where(position == 0, 0, jnp.where(position == 1, one, jnp.where(position == 2, 4 - one, 2)))


def layer(of_core, z, position):
    zz = z ^ offset(of_core, position)
    return ((zz // 2) * 2 + of_core) * 2 + zz % 2


def sum_kernel(where, grads, theirs, out, mine, other, sems):
    core, z, y, x = where[0], where[1], where[2], where[3]

    def load(i):
        rows = pl.ds(pl.multiple_of(layer(core, z, i) * 1024, 1024), 1024)
        return [
            pltpu.make_async_copy(grads.at[rows], mine.at[i % 2], sems.at[0, i % 2]),
            pltpu.make_async_copy(theirs.at[rows], other.at[i % 2], sems.at[1, i % 2]),
        ]

    for i in range(2):
        for copy in load(i):
            copy.start()
    for i in range(4):
        for copy in load(i):
            copy.wait()
        for b in range(4):
            for c in range(4):
                rows = pl.ds(pl.multiple_of((y ^ offset(core, b)) * 256 + (x ^ offset(core, c)) * 64, 64), 64)
                both = mine[i % 2, rows].astype(jnp.float32) + other[i % 2, rows].astype(jnp.float32)
                out[i, b, c] = both.astype(jnp.bfloat16)
        if i < 2:
            for copy in load(i + 2):
                copy.start()


def sum_grads(where, grads, theirs):
    columns = grads.shape[1]
    far = pl.BlockSpec(memory_space=pltpu.HBM)
    return pl.pallas_call(
        sum_kernel,
        out_shape=jax.ShapeDtypeStruct((4, 4, 4, 64, columns), jnp.bfloat16),
        in_specs=[pl.BlockSpec(memory_space=pltpu.SMEM), far, far],
        out_specs=pl.BlockSpec(memory_space=pltpu.VMEM),
        scratch_shapes=[
            pltpu.VMEM((2, 1024, columns), jnp.bfloat16),
            pltpu.VMEM((2, 1024, columns), jnp.bfloat16),
            pltpu.SemaphoreType.DMA((2, 2)),
        ],
        compiler_params=pltpu.CompilerParams(vmem_limit_bytes=40 * MIB),
        cost_estimate=pl.CostEstimate(flops=4096 * columns, bytes_accessed=24576 * columns, transcendentals=0),
        name="sum_grads",
    )(where, grads, theirs)


def project_kernel(late, summed, *refs):
    pieces, refs = refs[:3], refs[3:]
    if late:
        where, before, partial, sent, one, two, three, sems, out_sem = refs
    else:
        partial, one, two, three, sems = refs
    scratch = (one, two, three)
    loads = [
        [pltpu.make_async_copy(p.at[a], v.at[a], sems.at[s, a]) for a in range(p.shape[0])]
        for s, (p, v) in enumerate(zip(pieces, scratch))
    ]
    first = 2 if late else 0
    order = [(s, a) for s in range(3) for a in range(scratch[s].shape[0])]
    for s, a in order:
        loads[s][a].start()
    for s, a in order:
        loads[s][a].wait()
        low, high, axis = STREAMS[s]
        if axis == "x":
            rows = summed[a, :, first : first + 2]
        elif axis == "y":
            rows = summed[a, first : first + 2]
        else:
            rows = summed[first + a]
        depth = scratch[s].shape[1] * scratch[s].shape[2] * 64
        product = lax.dot_general(
            scratch[s][a].reshape(depth, high - low),
            rows.reshape(depth, rows.shape[-1]),
            (((0,), (0,)), ((), ())),
            preferred_element_type=jnp.float32,
        )
        if a > 0:
            partial[low:high] += product
        elif late:
            partial[low:high] = before[low:high] + product
        else:
            partial[low:high] = product
    if late:
        share = sent.shape[1]
        for far in range(2):
            row = pl.multiple_of((far * 2 + 1 - where[0]) * share, share)
            pltpu.make_async_copy(partial.at[pl.ds(row, share)], sent.at[far], out_sem).start()
        pltpu.make_async_copy(sent, sent, out_sem).wait()


def project(summed, pieces, where=None, before=None):
    columns = summed.shape[-1]
    late = before is not None
    anywhere, inside = pl.BlockSpec(memory_space=pl.ANY), pl.BlockSpec(memory_space=pltpu.VMEM)
    result = jax.ShapeDtypeStruct((1024, columns), jnp.float32)
    return pl.pallas_call(
        functools.partial(project_kernel, late),
        out_shape=(result, jax.ShapeDtypeStruct((2, 256, columns), jnp.float32)) if late else result,
        in_specs=[inside] + [anywhere] * 3 + [pl.BlockSpec(memory_space=pltpu.SMEM), inside] * late,
        out_specs=(inside, anywhere) if late else inside,
        scratch_shapes=[pltpu.VMEM(piece.shape, jnp.bfloat16) for piece in pieces]
        + [pltpu.SemaphoreType.DMA((3, 4))]
        + [pltpu.SemaphoreType.DMA] * late,
        compiler_params=pltpu.CompilerParams(vmem_limit_bytes=32 * MIB),
        cost_estimate=pl.CostEstimate(
            flops=summed.size * 1024, bytes_accessed=2 * summed.size + 4 * MIB, transcendentals=0
        ),
        name="project_late" if late else "project",
    )(summed, *pieces, *([where, before] if late else []))


def chip_kernel(where, partial, received, kept, sent):
    core, far = where[0], where[1] // 2
    share = kept.shape[0]

    def total(f):
        return partial[pl.ds(pl.multiple_of((f * 2 + core) * share, share), share)] + received[f]

    sent[...] = total(1 - far).astype(jnp.bfloat16)
    kept[...] = total(far)


def add_cores(where, partial, received):
    columns = partial.shape[1]
    inside = pl.BlockSpec(memory_space=pltpu.VMEM)
    return pl.pallas_call(
        chip_kernel,
        out_shape=(
            jax.ShapeDtypeStruct((256, columns), jnp.float32),
            jax.ShapeDtypeStruct((256, columns), jnp.bfloat16),
        ),
        in_specs=[pl.BlockSpec(memory_space=pltpu.SMEM), inside, inside],
        out_specs=(inside, inside),
        compiler_params=pltpu.CompilerParams(vmem_limit_bytes=16 * MIB),
        name="add_cores",
    )(where, partial, received)


def adam(kept, received, first_moment, second_moment):
    projected = (kept + received.astype(jnp.float32)) * (1.0 / 4)
    new_first = 0.9 * first_moment + 0.1 * projected
    new_second = 0.999 * second_moment + 0.001 * projected * projected
    return new_first, new_second


def direction_kernel(kept, received, first_moment, second_moment, out):
    new_first, new_second = adam(kept[...], received[...], first_moment[...], second_moment[...])
    out[...] = (new_first / first_fix / (jnp.sqrt(new_second / second_fix) + 1e-08)).astype(jnp.bfloat16)


def direct(*operands):
    inside = pl.BlockSpec(memory_space=pltpu.VMEM)
    return pl.pallas_call(
        direction_kernel,
        out_shape=jax.ShapeDtypeStruct(operands[0].shape, jnp.bfloat16),
        in_specs=[inside] * 4,
        out_specs=inside,
        compiler_params=pltpu.CompilerParams(vmem_limit_bytes=16 * MIB),
        name="direction",
    )(*operands)


SLOTS = 3


def update_kernel(where, *refs):
    bases, quarters, refs = (refs[:6], refs[6:12]), refs[12:16], refs[16:]
    out, direction, block, result, quarter_sem, in_sems, out_sems = refs
    core, z, y, x = where[0], where[1], where[2], where[3]

    def load(t):
        side, a = t // 4, t % 4
        slot = t % SLOTS
        for s, (low, high, axis) in enumerate(STREAMS):
            held, got = bases[side][2 * s], bases[side][2 * s + 1]
            if axis == "x":
                jobs = [(held, a, slice(None), pl.ds(0, 2)), (got, a, slice(None), pl.ds(2, 2))]
            elif axis == "y":
                jobs = [(held, a, pl.ds(0, 2), slice(None)), (got, a, pl.ds(2, 2), slice(None))]
            else:
                jobs = [(held if a < 2 else got, a % 2, slice(None), slice(None))]
            for source, index, b, c in jobs:
                pltpu.make_async_copy(
                    source.at[index], block.at[slot, b, c, :, pl.ds(low, high - low)], in_sems.at[slot]
                ).start()

    def drain(turn):
        pltpu.make_async_copy(result.at[turn], result.at[turn], out_sems.at[turn]).wait()

    far, share = z // 2, quarters[0].shape[0]
    for k, quarter in enumerate(quarters):
        place = (far ^ (k // 2)) * 2 + (core ^ (k % 2))
        rows = pl.ds(pl.multiple_of(place * share, share), share)
        pltpu.make_async_copy(quarter, direction.at[rows], quarter_sem).start()
    for t in range(SLOTS):
        load(t)
    pltpu.make_async_copy(direction, direction, quarter_sem).wait()
    for t in range(8):
        side, a = t // 4, t % 4
        of_core = core if side == 0 else 1 - core
        slot, turn = t % SLOTS, t % 2
        pltpu.make_async_copy(block.at[slot], block.at[slot], in_sems.at[slot]).wait()
        if t >= 2:
            drain(turn)
        result[turn] = jnp.dot(
            block[slot].reshape(1024, block.shape[-1]), direction[...], preferred_element_type=jnp.float32
        ).astype(jnp.bfloat16)
        if t + SLOTS < 8:
            load(t + SLOTS)
        base = layer(of_core, z, a) * 1024
        for b in range(4):
            for c in range(4):
                row = pl.multiple_of(base + (y ^ offset(of_core, b)) * 256 + (x ^ offset(of_core, c)) * 64, 64)
                pltpu.make_async_copy(
                    result.at[turn, pl.ds((b * 4 + c) * 64, 64)], out.at[pl.ds(row, 64)], out_sems.at[turn]
                ).start()
    drain(0)
    drain(1)


def back_project(where, bases, quarters):
    share, columns = quarters[0].shape
    rank = 4 * share
    rows = 2 * 4096
    anywhere = pl.BlockSpec(memory_space=pl.ANY)
    return pl.pallas_call(
        update_kernel,
        out_shape=jax.ShapeDtypeStruct((rows, columns), jnp.bfloat16),
        in_specs=[pl.BlockSpec(memory_space=pltpu.SMEM)] + [anywhere] * 16,
        out_specs=anywhere,
        scratch_shapes=[
            pltpu.VMEM((rank, columns), jnp.bfloat16),
            pltpu.VMEM((SLOTS, 4, 4, 64, rank), jnp.bfloat16),
            pltpu.VMEM((2, 1024, columns), jnp.bfloat16),
            pltpu.SemaphoreType.DMA,
            pltpu.SemaphoreType.DMA((SLOTS,)),
            pltpu.SemaphoreType.DMA((2,)),
        ],
        compiler_params=pltpu.CompilerParams(vmem_limit_bytes=32 * MIB),
        cost_estimate=pl.CostEstimate(
            flops=2 * rows * rank * columns, bytes_accessed=2 * rows * (rank + columns), transcendentals=0
        ),
        name="back_project",
    )(where, *bases, *quarters)


def local(grads, basis, first_moment, second_moment):
    dp, fsdp = lax.axis_index("dp"), lax.axis_index("fsdp")
    far, core = dp // 2, dp % 2
    z, y, x = far * 2 + fsdp // 16, (fsdp // 4) % 4, fsdp % 4
    where = jnp.stack([core, z, y, x]).astype(jnp.int32)

    whole = grads[0]
    columns = whole.shape[1]
    theirs = swap_core(whole)
    held = grow(grow(basis[None, None, None], "x", 0), "y", 0)
    wide, narrow = held[..., :768], held[..., 768:]
    wide, narrow = together(grow(wide, "z", 0), grow(narrow, "x", 1))
    wide, narrow = together(grow(wide, "z", 1), grow(narrow, "y", 1))
    halves = together(grow(wide[..., :384], "y", 1), grow(wide[..., 384:], "x", 1), grow(narrow, "z", 0))
    got = [exchange(half, axis, 1) for half, (_, _, axis) in zip(halves, STREAMS)]
    summed = sum_grads(where, whole, theirs)
    partial, sent = project(summed, got, where, project(summed, halves))

    kept, sent = add_cores(where, partial, swap_core(sent))
    received = swap_far(sent)
    direction = direct(kept, received, first_moment, second_moment)
    new_first, new_second = adam(kept, received, first_moment, second_moment)

    bases = []
    for half, late in zip(halves, got):
        bases += [half, late]
    bases += [swap_core(piece) for piece in bases]
    distant = swap_far(direction)
    update = back_project(where, bases, (direction, swap_core(direction), distant, swap_core(distant)))
    return (update, new_first, new_second)


def solution(mesh):
    return jax.shard_map(
        local,
        mesh=mesh,
        in_specs=(P("dp", None, "fsdp"), P(("dp", "fsdp"), None), P("dp", "fsdp"), P("dp", "fsdp")),
        out_specs=(P(None, "fsdp"), P("dp", "fsdp"), P("dp", "fsdp")),
        check_vma=False,
    )
```

```python
import functools
import math

import jax
import jax.numpy as jnp
from jax import lax
from jax.experimental import pallas as pl
from jax.experimental.pallas import tpu as pltpu
from jax.sharding import PartitionSpec as P

first_fix = 1.0 - math.exp(1000.0 * math.log(0.9))
second_fix = 1.0 - math.exp(1000.0 * math.log(0.999))

BOTH = ("dp", "fsdp")
ORDER = ((0, 3, 1, 2), (0, 1, 3, 2))
STREAMS = ((0, 384, "yzx"), (384, 768, "zxy"), (768, 1024, "xyz"))
MIB = 1024 * 1024


def linear(c, z, y, x):
    return (((z // 2) * 2 + c) * 2 + z % 2) * 16 + y * 4 + x


def pairs(partner):
    return [
        (linear(c, z, y, x), linear(*partner(c, z, y, x)))
        for c in range(2)
        for z in range(4)
        for y in range(4)
        for x in range(4)
    ]


def exchange(value, axes, step):
    def partner(c, z, y, x):
        t = ORDER[c][1] if step == 0 else ORDER[1 - c][1]
        return c, z ^ t if "z" in axes else z, y ^ t if "y" in axes else y, x ^ t if "x" in axes else x

    return lax.ppermute(value, BOTH, pairs(partner))


def swap_core(value):
    return lax.ppermute(value, BOTH, pairs(lambda c, z, y, x: (1 - c, z, y, x)))


def swap_far(value):
    return lax.ppermute(value, BOTH, pairs(lambda c, z, y, x: (c, z ^ 2, y, x)))


def cube(shard):
    x, y, xy = together(*[exchange(shard, axes, 0) for axes in ("x", "y", "xy")])
    square = jnp.stack([shard, x, y, xy])
    return x, jnp.concatenate([square, exchange(square, "z", 0)]).reshape(2, 2, 2, *shard.shape)


def grow(held, axis):
    return jnp.concatenate([held, exchange(held, axis, 1)], axis="zyx".index(axis))


def corner(axes, quarter):
    out = []
    for axis in "zyx":
        late = quarter % 2 if axis == axes[1] else quarter // 2
        out.append(slice(0, 4) if axis == axes[0] else slice(2 * late, 2 * late + 2))
    return tuple(out)


def bring_kernel(source, out, sem):
    copy = pltpu.make_async_copy(source, out, sem)
    copy.start()
    copy.wait()


def bring(value):
    return pl.pallas_call(
        bring_kernel,
        out_shape=jax.ShapeDtypeStruct(value.shape, value.dtype),
        in_specs=[pl.BlockSpec(memory_space=pl.ANY)],
        out_specs=pl.BlockSpec(memory_space=pltpu.VMEM),
        scratch_shapes=[pltpu.SemaphoreType.DMA],
        compiler_params=pltpu.CompilerParams(vmem_limit_bytes=4 * MIB),
        name="bring",
    )(value)


def together(*values):
    return lax.optimization_barrier(values)


def offset(of_core, position):
    one = jnp.where(of_core == 0, 3, 1)
    return jnp.where(position == 0, 0, jnp.where(position == 1, one, jnp.where(position == 2, 4 - one, 2)))


def layer(of_core, z, position):
    zz = z ^ offset(of_core, position)
    return ((zz // 2) * 2 + of_core) * 2 + zz % 2


def sum_kernel(where, grads, theirs, out, mine, other, sems):
    core, z, y, x = where[0], where[1], where[2], where[3]

    def load(i):
        rows = pl.ds(pl.multiple_of(layer(core, z, i) * 1024, 1024), 1024)
        return [
            pltpu.make_async_copy(grads.at[rows], mine.at[i % 2], sems.at[0, i % 2]),
            pltpu.make_async_copy(theirs.at[rows], other.at[i % 2], sems.at[1, i % 2]),
        ]

    for i in range(2):
        for copy in load(i):
            copy.start()
    for i in range(4):
        for copy in load(i):
            copy.wait()
        for b in range(4):
            for c in range(4):
                rows = pl.ds(pl.multiple_of((y ^ offset(core, b)) * 256 + (x ^ offset(core, c)) * 64, 64), 64)
                both = mine[i % 2, rows].astype(jnp.float32) + other[i % 2, rows].astype(jnp.float32)
                out[i, b, c] = both.astype(jnp.bfloat16)
        if i < 2:
            for copy in load(i + 2):
                copy.start()


def sum_grads(where, grads, theirs):
    columns = grads.shape[1]
    far = pl.BlockSpec(memory_space=pltpu.HBM)
    return pl.pallas_call(
        sum_kernel,
        out_shape=jax.ShapeDtypeStruct((4, 4, 4, 64, columns), jnp.bfloat16),
        in_specs=[pl.BlockSpec(memory_space=pltpu.SMEM), far, far],
        out_specs=pl.BlockSpec(memory_space=pltpu.VMEM),
        scratch_shapes=[
            pltpu.VMEM((2, 1024, columns), jnp.bfloat16),
            pltpu.VMEM((2, 1024, columns), jnp.bfloat16),
            pltpu.SemaphoreType.DMA((2, 2)),
        ],
        compiler_params=pltpu.CompilerParams(vmem_limit_bytes=40 * MIB),
        cost_estimate=pl.CostEstimate(flops=4096 * columns, bytes_accessed=24576 * columns, transcendentals=0),
        name="sum_grads",
    )(where, grads, theirs)


def project_kernel(late, summed, *refs):
    pieces, refs = refs[:6], refs[6:]
    if late:
        where, before, partial, sent, *scratch, sems, out_sem = refs
    else:
        partial, *scratch, sems = refs
    loads = [pltpu.make_async_copy(p, v, sems.at[k]) for k, (p, v) in enumerate(zip(pieces, scratch))]
    for load in loads:
        load.start()
    for k, load in enumerate(loads):
        load.wait()
        low, high, axes = STREAMS[k // 2]
        z, y, x = corner(axes, 2 * late + k % 2)
        rows = summed[z, y, x]
        product = lax.dot_general(
            scratch[k][...].reshape(1024, high - low),
            rows.reshape(1024, rows.shape[-1]),
            (((0,), (0,)), ((), ())),
            preferred_element_type=jnp.float32,
        )
        if k % 2:
            partial[low:high] += product
        elif late:
            partial[low:high] = before[low:high] + product
        else:
            partial[low:high] = product
    if late:
        share = sent.shape[1]
        for far in range(2):
            row = pl.multiple_of((far * 2 + 1 - where[0]) * share, share)
            pltpu.make_async_copy(partial.at[pl.ds(row, share)], sent.at[far], out_sem).start()
        pltpu.make_async_copy(sent, sent, out_sem).wait()


def project(summed, pieces, where=None, before=None):
    columns = summed.shape[-1]
    late = before is not None
    anywhere, inside = pl.BlockSpec(memory_space=pl.ANY), pl.BlockSpec(memory_space=pltpu.VMEM)
    result = jax.ShapeDtypeStruct((1024, columns), jnp.float32)
    return pl.pallas_call(
        functools.partial(project_kernel, late),
        out_shape=(result, jax.ShapeDtypeStruct((2, 256, columns), jnp.float32)) if late else result,
        in_specs=[inside] + [anywhere] * 6 + [pl.BlockSpec(memory_space=pltpu.SMEM), inside] * late,
        out_specs=(inside, anywhere) if late else inside,
        scratch_shapes=[pltpu.VMEM(piece.shape, jnp.bfloat16) for piece in pieces]
        + [pltpu.SemaphoreType.DMA((6,))]
        + [pltpu.SemaphoreType.DMA] * late,
        compiler_params=pltpu.CompilerParams(vmem_limit_bytes=32 * MIB),
        cost_estimate=pl.CostEstimate(
            flops=summed.size * 1024, bytes_accessed=2 * summed.size + 4 * MIB, transcendentals=0
        ),
        name="project_late" if late else "project",
    )(summed, *pieces, *([where, before] if late else []))


def chip_kernel(where, partial, received, kept, sent):
    core, far = where[0], where[1] // 2
    share = kept.shape[0]

    def total(f):
        return partial[pl.ds(pl.multiple_of((f * 2 + core) * share, share), share)] + received[f]

    sent[...] = total(1 - far).astype(jnp.bfloat16)
    kept[...] = total(far)


def add_cores(where, partial, received):
    columns = partial.shape[1]
    inside = pl.BlockSpec(memory_space=pltpu.VMEM)
    return pl.pallas_call(
        chip_kernel,
        out_shape=(
            jax.ShapeDtypeStruct((256, columns), jnp.float32),
            jax.ShapeDtypeStruct((256, columns), jnp.bfloat16),
        ),
        in_specs=[pl.BlockSpec(memory_space=pltpu.SMEM), inside, inside],
        out_specs=(inside, inside),
        compiler_params=pltpu.CompilerParams(vmem_limit_bytes=16 * MIB),
        name="add_cores",
    )(where, partial, received)


def adam(kept, received, first_moment, second_moment):
    projected = (kept + received.astype(jnp.float32)) * (1.0 / 4)
    new_first = 0.9 * first_moment + 0.1 * projected
    new_second = 0.999 * second_moment + 0.001 * projected * projected
    return new_first, new_second


def direction_kernel(kept, received, first_moment, second_moment, out):
    new_first, new_second = adam(kept[...], received[...], first_moment[...], second_moment[...])
    out[...] = (new_first / first_fix / (jnp.sqrt(new_second / second_fix) + 1e-08)).astype(jnp.bfloat16)


def direct(*operands):
    inside = pl.BlockSpec(memory_space=pltpu.VMEM)
    return pl.pallas_call(
        direction_kernel,
        out_shape=jax.ShapeDtypeStruct(operands[0].shape, jnp.bfloat16),
        in_specs=[inside] * 4,
        out_specs=inside,
        compiler_params=pltpu.CompilerParams(vmem_limit_bytes=16 * MIB),
        name="direction",
    )(*operands)


SLOTS = 3


def update_kernel(where, *refs):
    bases, quarters, refs = (refs[:12], refs[12:24]), refs[24:28], refs[28:]
    out, direction, block, result, in_sems, out_sems = refs
    core, z, y, x = where[0], where[1], where[2], where[3]

    def load(t):
        side, a = t // 4, t % 4
        slot = t % SLOTS
        for k, piece in enumerate(bases[side]):
            low, high, axes = STREAMS[k // 4]
            layers, b, c = corner(axes, k % 4)
            if layers.start <= a < layers.stop:
                pltpu.make_async_copy(
                    piece.at[a - layers.start],
                    block.at[slot, pl.ds(b.start, b.stop - b.start), pl.ds(c.start, c.stop - c.start), :, pl.ds(low, high - low)],
                    in_sems.at[slot],
                ).start()

    def drain(turn):
        pltpu.make_async_copy(result.at[turn], result.at[turn], out_sems.at[turn]).wait()

    for t in range(SLOTS):
        load(t)
    far, share = z // 2, quarters[0].shape[0]
    for k, quarter in enumerate(quarters):
        place = (far ^ (k // 2)) * 2 + (core ^ (k % 2))
        direction[pl.ds(pl.multiple_of(place * share, share), share)] = quarter[...]
    for t in range(8):
        side, a = t // 4, t % 4
        of_core = core if side == 0 else 1 - core
        slot, turn = t % SLOTS, t % 2
        pltpu.make_async_copy(block.at[slot], block.at[slot], in_sems.at[slot]).wait()
        if t >= 2:
            drain(turn)
        result[turn] = jnp.dot(
            block[slot].reshape(1024, block.shape[-1]), direction[...], preferred_element_type=jnp.float32
        ).astype(jnp.bfloat16)
        if t + SLOTS < 8:
            load(t + SLOTS)
        base = layer(of_core, z, a) * 1024
        for b in range(4):
            for c in range(4):
                row = pl.multiple_of(base + (y ^ offset(of_core, b)) * 256 + (x ^ offset(of_core, c)) * 64, 64)
                pltpu.make_async_copy(
                    result.at[turn, pl.ds((b * 4 + c) * 64, 64)], out.at[pl.ds(row, 64)], out_sems.at[turn]
                ).start()
    drain(0)
    drain(1)


def back_project(where, bases, quarters):
    share, columns = quarters[0].shape
    rank = 4 * share
    rows = 2 * 4096
    anywhere, inside = pl.BlockSpec(memory_space=pl.ANY), pl.BlockSpec(memory_space=pltpu.VMEM)
    return pl.pallas_call(
        update_kernel,
        out_shape=jax.ShapeDtypeStruct((rows, columns), jnp.bfloat16),
        in_specs=[pl.BlockSpec(memory_space=pltpu.SMEM)] + [anywhere] * 24 + [inside] * 4,
        out_specs=anywhere,
        scratch_shapes=[
            pltpu.VMEM((rank, columns), jnp.bfloat16),
            pltpu.VMEM((SLOTS, 4, 4, 64, rank), jnp.bfloat16),
            pltpu.VMEM((2, 1024, columns), jnp.bfloat16),
            pltpu.SemaphoreType.DMA((SLOTS,)),
            pltpu.SemaphoreType.DMA((2,)),
        ],
        compiler_params=pltpu.CompilerParams(vmem_limit_bytes=32 * MIB),
        cost_estimate=pl.CostEstimate(
            flops=2 * rows * rank * columns, bytes_accessed=2 * rows * (rank + columns), transcendentals=0
        ),
        name="back_project",
    )(where, *bases, *quarters)


def local(grads, basis, first_moment, second_moment):
    dp, fsdp = lax.axis_index("dp"), lax.axis_index("fsdp")
    far, core = dp // 2, dp % 2
    z, y, x = far * 2 + fsdp // 16, (fsdp // 4) % 4, fsdp % 4
    where = jnp.stack([core, z, y, x]).astype(jnp.int32)

    whole = grads[0]
    columns = whole.shape[1]
    shard = bring(basis)
    first, held = cube(shard)
    first, whole = together(first, whole)
    theirs = swap_core(whole)
    (held,) = together(held)
    halves = [held[..., low:high] for low, high, _ in STREAMS]
    *halves, theirs = together(*[grow(half, axes[0]) for half, (_, _, axes) in zip(halves, STREAMS)], theirs)
    second = [exchange(half, axes[1], 1) for half, (_, _, axes) in zip(halves, STREAMS)]
    third = [exchange(half, axes[2], 1) for half, (_, _, axes) in zip(halves, STREAMS)]
    fourth = [exchange(got, axes[2], 1) for got, (_, _, axes) in zip(second, STREAMS)]
    early = [piece for pair in zip(halves, second) for piece in pair]
    late = [piece for pair in zip(third, fourth) for piece in pair]
    summed = sum_grads(where, whole, theirs)
    *ready, summed = together(*early, summed)
    swapped = [swap_core(piece) for piece in ready]
    partial, sent = project(summed, late, where, project(summed, early))

    kept, sent = add_cores(where, partial, swap_core(sent))
    received, *waiting = together(swap_far(sent), *late)
    direction = direct(kept, received, first_moment, second_moment)
    new_first, new_second = adam(kept, received, first_moment, second_moment)

    waiting = [swap_core(piece) for piece in waiting]

    def arranged(first, last):
        return [piece for k in range(3) for piece in (*first[2 * k : 2 * k + 2], *last[2 * k : 2 * k + 2])]

    own, other = arranged(early, late), arranged(swapped, waiting)
    distant = swap_far(direction)
    update = back_project(where, own + other, (direction, swap_core(direction), distant, swap_core(distant)))
    return (update, new_first, new_second)


def solution(mesh):
    return jax.shard_map(
        local,
        mesh=mesh,
        in_specs=(P("dp", None, "fsdp"), P(("dp", "fsdp"), None), P("dp", "fsdp"), P("dp", "fsdp")),
        out_specs=(P(None, "fsdp"), P("dp", "fsdp"), P("dp", "fsdp")),
        check_vma=False,
    )
```

```python
import functools
import math

import jax
import jax.numpy as jnp
from jax import lax
from jax.experimental import pallas as pl
from jax.experimental.pallas import tpu as pltpu
from jax.sharding import PartitionSpec as P

first_fix = 1.0 - math.exp(1000.0 * math.log(0.9))
second_fix = 1.0 - math.exp(1000.0 * math.log(0.999))

BOTH = ("dp", "fsdp")
ORDER = ((0, 3, 1, 2), (0, 1, 3, 2))
STREAMS = ((0, 384, "yzx"), (384, 768, "zxy"), (768, 1024, "xyz"))
MIB = 1024 * 1024


def linear(c, z, y, x):
    return (((z // 2) * 2 + c) * 2 + z % 2) * 16 + y * 4 + x


def pairs(partner):
    return [
        (linear(c, z, y, x), linear(*partner(c, z, y, x)))
        for c in range(2)
        for z in range(4)
        for y in range(4)
        for x in range(4)
    ]


def exchange(value, axes, step):
    def partner(c, z, y, x):
        t, u = (ORDER[c][1], ORDER[1 - c][1]) if step == 0 else (ORDER[1 - c][1], ORDER[c][1])
        return c, z ^ u if "z" in axes else z, y ^ t if "y" in axes else y, x ^ t if "x" in axes else x

    return lax.ppermute(value, BOTH, pairs(partner))


def swap_core(value):
    return lax.ppermute(value, BOTH, pairs(lambda c, z, y, x: (1 - c, z, y, x)))


def swap_far(value):
    return lax.ppermute(value, BOTH, pairs(lambda c, z, y, x: (c, z ^ 2, y, x)))


def bring_kernel(source, out, sem):
    copy = pltpu.make_async_copy(source, out, sem)
    copy.start()
    copy.wait()


def bring(value):
    return pl.pallas_call(
        bring_kernel,
        out_shape=jax.ShapeDtypeStruct(value.shape, value.dtype),
        in_specs=[pl.BlockSpec(memory_space=pl.ANY)],
        out_specs=pl.BlockSpec(memory_space=pltpu.VMEM),
        scratch_shapes=[pltpu.SemaphoreType.DMA],
        compiler_params=pltpu.CompilerParams(vmem_limit_bytes=4 * MIB),
        name="bring",
    )(value)


def cube(shard):
    x, y, xy, z = together(*[exchange(shard, axes, 0) for axes in ("x", "y", "xy", "z")])
    xz, yz, xyz = exchange(jnp.stack([x, y, xy]), "z", 0)
    return jnp.stack([bring(shard), x, y, xy, z, xz, yz, xyz]).reshape(2, 2, 2, *shard.shape)


def join(first, second, axis):
    return jnp.concatenate([first, second], axis="zyx".index(axis))


def corner(axes, quarter):
    out = []
    for axis in "zyx":
        late = quarter % 2 if axis == axes[1] else quarter // 2
        out.append(slice(0, 4) if axis == axes[0] else slice(2 * late, 2 * late + 2))
    return tuple(out)


def together(*values):
    return lax.optimization_barrier(values)


def offset(of_core, position):
    one = jnp.where(of_core == 0, 3, 1)
    return jnp.where(position == 0, 0, jnp.where(position == 1, one, jnp.where(position == 2, 4 - one, 2)))


def layer(of_core, z, position):
    zz = z ^ offset(1 - of_core, position)
    return ((zz // 2) * 2 + of_core) * 2 + zz % 2


def sum_kernel(where, grads, theirs, out, mine, other, sems):
    core, z, y, x = where[0], where[1], where[2], where[3]

    def load(i):
        rows = pl.ds(pl.multiple_of(layer(core, z, i) * 1024, 1024), 1024)
        return [
            pltpu.make_async_copy(grads.at[rows], mine.at[i % 2], sems.at[0, i % 2]),
            pltpu.make_async_copy(theirs.at[rows], other.at[i % 2], sems.at[1, i % 2]),
        ]

    for i in range(2):
        for copy in load(i):
            copy.start()
    for i in range(4):
        for copy in load(i):
            copy.wait()
        for b in range(4):
            for c in range(4):
                rows = pl.ds(pl.multiple_of((y ^ offset(core, b)) * 256 + (x ^ offset(core, c)) * 64, 64), 64)
                both = mine[i % 2, rows].astype(jnp.float32) + other[i % 2, rows].astype(jnp.float32)
                out[i, b, c] = both.astype(jnp.bfloat16)
        if i < 2:
            for copy in load(i + 2):
                copy.start()


def sum_grads(where, grads, theirs):
    columns = grads.shape[1]
    far = pl.BlockSpec(memory_space=pltpu.HBM)
    return pl.pallas_call(
        sum_kernel,
        out_shape=jax.ShapeDtypeStruct((4, 4, 4, 64, columns), jnp.bfloat16),
        in_specs=[pl.BlockSpec(memory_space=pltpu.SMEM), far, far],
        out_specs=pl.BlockSpec(memory_space=pltpu.VMEM),
        scratch_shapes=[
            pltpu.VMEM((2, 1024, columns), jnp.bfloat16),
            pltpu.VMEM((2, 1024, columns), jnp.bfloat16),
            pltpu.SemaphoreType.DMA((2, 2)),
        ],
        compiler_params=pltpu.CompilerParams(vmem_limit_bytes=40 * MIB),
        cost_estimate=pl.CostEstimate(flops=4096 * columns, bytes_accessed=24576 * columns, transcendentals=0),
        name="sum_grads",
    )(where, grads, theirs)


def project_kernel(late, summed, *refs):
    pieces, refs = refs[:6], refs[6:]
    if late:
        where, before, partial, sent, *refs = refs
    else:
        partial, *refs = refs
    packed, scratch, (sems, pack_sem, out_sem) = refs[:3], refs[3:9], refs[9:]
    loads = [pltpu.make_async_copy(p, v, sems.at[k]) for k, (p, v) in enumerate(zip(pieces, scratch))]
    for load in loads:
        load.start()
    for k, load in enumerate(loads):
        load.wait()
        pltpu.make_async_copy(scratch[k], packed[k // 2].at[k % 2], pack_sem).start()
        low, high, axes = STREAMS[k // 2]
        z, y, x = corner(axes, 2 * late + k % 2)
        rows = summed[z, y, x]
        product = lax.dot_general(
            scratch[k][...].reshape(1024, high - low),
            rows.reshape(1024, rows.shape[-1]),
            (((0,), (0,)), ((), ())),
            preferred_element_type=jnp.float32,
        )
        if k % 2:
            partial[low:high] += product
        elif late:
            partial[low:high] = before[low:high] + product
        else:
            partial[low:high] = product
    if late:
        share = sent.shape[1]
        for far in range(2):
            row = pl.multiple_of((far * 2 + 1 - where[0]) * share, share)
            pltpu.make_async_copy(partial.at[pl.ds(row, share)], sent.at[far], out_sem).start()
        pltpu.make_async_copy(sent, sent, out_sem).wait()
    for out in packed:
        pltpu.make_async_copy(out, out, pack_sem).wait()


def project(summed, pieces, where=None, before=None):
    columns = summed.shape[-1]
    late = before is not None
    anywhere, inside = pl.BlockSpec(memory_space=pl.ANY), pl.BlockSpec(memory_space=pltpu.VMEM)
    result = [jax.ShapeDtypeStruct((1024, columns), jnp.float32)]
    if late:
        result.append(jax.ShapeDtypeStruct((2, 256, columns), jnp.float32))
    packed = [jax.ShapeDtypeStruct((2, *piece.shape), piece.dtype) for piece in pieces[::2]]
    return pl.pallas_call(
        functools.partial(project_kernel, late),
        out_shape=result + packed,
        in_specs=[inside] + [anywhere] * 6 + [pl.BlockSpec(memory_space=pltpu.SMEM), inside] * late,
        out_specs=[inside] + [anywhere] * (len(result) + 2),
        scratch_shapes=[pltpu.VMEM(piece.shape, jnp.bfloat16) for piece in pieces]
        + [pltpu.SemaphoreType.DMA((6,)), pltpu.SemaphoreType.DMA, pltpu.SemaphoreType.DMA],
        compiler_params=pltpu.CompilerParams(vmem_limit_bytes=32 * MIB),
        cost_estimate=pl.CostEstimate(
            flops=summed.size * 1024, bytes_accessed=2 * summed.size + 4 * MIB, transcendentals=0
        ),
        name="project_late" if late else "project",
    )(summed, *pieces, *([where, before] if late else []))


def chip_kernel(where, partial, received, kept, sent):
    core, far = where[0], where[1] // 2
    share = kept.shape[0]

    def total(f):
        return partial[pl.ds(pl.multiple_of((f * 2 + core) * share, share), share)] + received[f]

    sent[...] = total(1 - far).astype(jnp.bfloat16)
    kept[...] = total(far)


def add_cores(where, partial, received):
    columns = partial.shape[1]
    inside = pl.BlockSpec(memory_space=pltpu.VMEM)
    return pl.pallas_call(
        chip_kernel,
        out_shape=(
            jax.ShapeDtypeStruct((256, columns), jnp.float32),
            jax.ShapeDtypeStruct((256, columns), jnp.bfloat16),
        ),
        in_specs=[pl.BlockSpec(memory_space=pltpu.SMEM), inside, inside],
        out_specs=(inside, inside),
        compiler_params=pltpu.CompilerParams(vmem_limit_bytes=16 * MIB),
        name="add_cores",
    )(where, partial, received)


def adam(kept, received, first_moment, second_moment):
    projected = (kept + received.astype(jnp.float32)) * (1.0 / 4)
    new_first = 0.9 * first_moment + 0.1 * projected
    new_second = 0.999 * second_moment + 0.001 * projected * projected
    return new_first, new_second


def direction_kernel(kept, received, first_moment, second_moment, out):
    new_first, new_second = adam(kept[...], received[...], first_moment[...], second_moment[...])
    out[...] = (new_first / first_fix / (jnp.sqrt(new_second / second_fix) + 1e-08)).astype(jnp.bfloat16)


def direct(*operands):
    inside = pl.BlockSpec(memory_space=pltpu.VMEM)
    return pl.pallas_call(
        direction_kernel,
        out_shape=jax.ShapeDtypeStruct(operands[0].shape, jnp.bfloat16),
        in_specs=[inside] * 4,
        out_specs=inside,
        compiler_params=pltpu.CompilerParams(vmem_limit_bytes=16 * MIB),
        name="direction",
    )(*operands)


SLOTS = 3


def update_kernel(where, *refs):
    own, other, quarters, refs = refs[:12], refs[12:18], refs[18:22], refs[22:]
    bases = own, [other[2 * (k // 4) + (k % 4) // 2].at[k % 2] for k in range(12)]
    out, direction, block, result, in_sems, out_sems = refs
    core, z, y, x = where[0], where[1], where[2], where[3]

    def load(t):
        side, a = t // 4, t % 4
        slot = t % SLOTS
        for k, piece in enumerate(bases[side]):
            low, high, axes = STREAMS[k // 4]
            layers, b, c = corner(axes, k % 4)
            if layers.start <= a < layers.stop:
                pltpu.make_async_copy(
                    piece.at[a - layers.start],
                    block.at[slot, pl.ds(b.start, b.stop - b.start), pl.ds(c.start, c.stop - c.start), :, pl.ds(low, high - low)],
                    in_sems.at[slot],
                ).start()

    def drain(turn):
        pltpu.make_async_copy(result.at[turn], result.at[turn], out_sems.at[turn]).wait()

    for t in range(SLOTS):
        load(t)
    far, share = z // 2, quarters[0].shape[0]
    for k, quarter in enumerate(quarters):
        place = (far ^ (k // 2)) * 2 + (core ^ (k % 2))
        direction[pl.ds(pl.multiple_of(place * share, share), share)] = quarter[...]
    for t in range(8):
        side, a = t // 4, t % 4
        of_core = core if side == 0 else 1 - core
        slot, turn = t % SLOTS, t % 2
        pltpu.make_async_copy(block.at[slot], block.at[slot], in_sems.at[slot]).wait()
        if t >= 2:
            drain(turn)
        base = layer(of_core, z, a) * 1024
        parts = 1 if t < 7 else 2
        for b in range(4):
            if b % (4 // parts) == 0:
                size = 1024 // parts
                result[turn, b * 256 : b * 256 + size] = jnp.dot(
                    block[slot, b : b + 4 // parts].reshape(size, block.shape[-1]),
                    direction[...],
                    preferred_element_type=jnp.float32,
                ).astype(jnp.bfloat16)
            if b == 0 and t + SLOTS < 8:
                load(t + SLOTS)
            for c in range(4):
                row = pl.multiple_of(base + (y ^ offset(of_core, b)) * 256 + (x ^ offset(of_core, c)) * 64, 64)
                pltpu.make_async_copy(
                    result.at[turn, pl.ds((b * 4 + c) * 64, 64)], out.at[pl.ds(row, 64)], out_sems.at[turn]
                ).start()
    drain(0)
    drain(1)


def back_project(where, bases, quarters):
    share, columns = quarters[0].shape
    rank = 4 * share
    rows = 2 * 4096
    anywhere, inside = pl.BlockSpec(memory_space=pl.ANY), pl.BlockSpec(memory_space=pltpu.VMEM)
    return pl.pallas_call(
        update_kernel,
        out_shape=jax.ShapeDtypeStruct((rows, columns), jnp.bfloat16),
        in_specs=[pl.BlockSpec(memory_space=pltpu.SMEM)] + [anywhere] * 18 + [inside] * 4,
        out_specs=anywhere,
        scratch_shapes=[
            pltpu.VMEM((rank, columns), jnp.bfloat16),
            pltpu.VMEM((SLOTS, 4, 4, 64, rank), jnp.bfloat16),
            pltpu.VMEM((2, 1024, columns), jnp.bfloat16),
            pltpu.SemaphoreType.DMA((SLOTS,)),
            pltpu.SemaphoreType.DMA((2,)),
        ],
        compiler_params=pltpu.CompilerParams(vmem_limit_bytes=32 * MIB),
        cost_estimate=pl.CostEstimate(
            flops=2 * rows * rank * columns, bytes_accessed=2 * rows * (rank + columns), transcendentals=0
        ),
        name="back_project",
    )(where, *bases, *quarters)


def local(grads, basis, first_moment, second_moment):
    dp, fsdp = lax.axis_index("dp"), lax.axis_index("fsdp")
    far, core = dp // 2, dp % 2
    z, y, x = far * 2 + fsdp // 16, (fsdp // 4) % 4, fsdp % 4
    where = jnp.stack([core, z, y, x]).astype(jnp.int32)

    whole = grads[0]
    columns = whole.shape[1]
    theirs = swap_core(whole)
    held, theirs = together(cube(basis), theirs)
    eighths = [held[..., low:high] for low, high, _ in STREAMS]
    got = [exchange(eighth, axes[0], 1) for eighth, (_, _, axes) in zip(eighths, STREAMS)]
    ahead = [exchange(eighth, axes[1], 1) for eighth, (_, _, axes) in zip(eighths, STREAMS)]
    got = together(*got)
    halves = [join(eighth, other, axes[0]) for eighth, other, (_, _, axes) in zip(eighths, got, STREAMS)]
    behind = [exchange(other, axes[1], 1) for other, (_, _, axes) in zip(got, STREAMS)]
    third = [exchange(half, axes[2], 1) for half, (_, _, axes) in zip(halves, STREAMS)]
    second = [join(first, last, axes[0]) for first, last, (_, _, axes) in zip(ahead, behind, STREAMS)]
    fourth = [exchange(got, axes[2], 1) for got, (_, _, axes) in zip(second, STREAMS)]
    early = [piece for pair in zip(halves, second) for piece in pair]
    late = [piece for pair in zip(third, fourth) for piece in pair]
    summed = sum_grads(where, whole, theirs)
    partial, *packed = project(summed, early)
    partial, sent, *more = project(summed, late, where, partial)

    kept, sent = add_cores(where, partial, swap_core(sent))
    kept, *more = together(kept, *more)
    received = swap_far(sent)
    direction = direct(kept, received, first_moment, second_moment)
    new_first, new_second = adam(kept, received, first_moment, second_moment)

    distant = swap_far(direction)
    near = swap_core(direction)
    own = [piece for k in range(3) for piece in (*early[2 * k : 2 * k + 2], *late[2 * k : 2 * k + 2])]
    other = [swap_core(value) for pair in zip(packed, more) for value in pair]
    update = back_project(where, own + other, (direction, near, distant, swap_core(distant)))
    return (update, new_first, new_second)


def solution(mesh):
    return jax.shard_map(
        local,
        mesh=mesh,
        in_specs=(P("dp", None, "fsdp"), P(("dp", "fsdp"), None), P("dp", "fsdp"), P("dp", "fsdp")),
        out_specs=(P(None, "fsdp"), P("dp", "fsdp"), P("dp", "fsdp")),
        check_vma=False,
    )
```

```python
import functools
import math

import jax
import jax.numpy as jnp
from jax import lax
from jax.experimental import pallas as pl
from jax.experimental.pallas import tpu as pltpu
from jax.sharding import PartitionSpec as P

first_fix = 1.0 - math.exp(1000.0 * math.log(0.9))
second_fix = 1.0 - math.exp(1000.0 * math.log(0.999))

BOTH = ("dp", "fsdp")
ORDER = ((0, 3, 1, 2), (0, 1, 3, 2))
STREAMS = ((0, 384, "yzx"), (384, 768, "zxy"), (768, 1024, "xyz"))
MIB = 1024 * 1024


def linear(c, z, y, x):
    return (((z // 2) * 2 + c) * 2 + z % 2) * 16 + y * 4 + x


def pairs(partner):
    return [
        (linear(c, z, y, x), linear(*partner(c, z, y, x)))
        for c in range(2)
        for z in range(4)
        for y in range(4)
        for x in range(4)
    ]


def exchange(value, axes, step):
    def partner(c, z, y, x):
        t, u = (ORDER[c][1], ORDER[1 - c][1]) if step == 0 else (ORDER[1 - c][1], ORDER[c][1])
        return c, z ^ u if "z" in axes else z, y ^ t if "y" in axes else y, x ^ t if "x" in axes else x

    return lax.ppermute(value, BOTH, pairs(partner))


def swap_core(value):
    return lax.ppermute(value, BOTH, pairs(lambda c, z, y, x: (1 - c, z, y, x)))


def swap_far(value):
    return lax.ppermute(value, BOTH, pairs(lambda c, z, y, x: (c, z ^ 2, y, x)))


def bring_kernel(source, out, sem):
    copy = pltpu.make_async_copy(source, out, sem)
    copy.start()
    copy.wait()


def bring(value):
    return pl.pallas_call(
        bring_kernel,
        out_shape=jax.ShapeDtypeStruct(value.shape, value.dtype),
        in_specs=[pl.BlockSpec(memory_space=pl.ANY)],
        out_specs=pl.BlockSpec(memory_space=pltpu.VMEM),
        scratch_shapes=[pltpu.SemaphoreType.DMA],
        compiler_params=pltpu.CompilerParams(vmem_limit_bytes=4 * MIB),
        name="bring",
    )(value)


def cube(shard):
    x, y, xy, z = together(*[exchange(shard, axes, 0) for axes in ("x", "y", "xy", "z")])
    xz, yz, xyz = exchange(jnp.stack([x, y, xy]), "z", 0)
    return jnp.stack([bring(shard), x, y, xy, z, xz, yz, xyz]).reshape(2, 2, 2, *shard.shape)


def join(first, second, axis):
    return jnp.concatenate([first, second], axis="zyx".index(axis))


def corner(axes, quarter):
    out = []
    for axis in "zyx":
        late = quarter % 2 if axis == axes[1] else quarter // 2
        out.append(slice(0, 4) if axis == axes[0] else slice(2 * late, 2 * late + 2))
    return tuple(out)


def together(*values):
    return lax.optimization_barrier(values)


def offset(of_core, position):
    one = jnp.where(of_core == 0, 3, 1)
    return jnp.where(position == 0, 0, jnp.where(position == 1, one, jnp.where(position == 2, 4 - one, 2)))


def layer(of_core, z, position):
    zz = z ^ offset(1 - of_core, position)
    return ((zz // 2) * 2 + of_core) * 2 + zz % 2


def sum_kernel(where, grads, theirs, out, mine, other, sems):
    core, z, y, x = where[0], where[1], where[2], where[3]

    def load(i):
        rows = pl.ds(pl.multiple_of(layer(core, z, i) * 1024, 1024), 1024)
        return [
            pltpu.make_async_copy(grads.at[rows], mine.at[i % 2], sems.at[0, i % 2]),
            pltpu.make_async_copy(theirs.at[rows], other.at[i % 2], sems.at[1, i % 2]),
        ]

    for i in range(2):
        for copy in load(i):
            copy.start()
    for i in range(4):
        for copy in load(i):
            copy.wait()
        for b in range(4):
            for c in range(4):
                rows = pl.ds(pl.multiple_of((y ^ offset(core, b)) * 256 + (x ^ offset(core, c)) * 64, 64), 64)
                both = mine[i % 2, rows].astype(jnp.float32) + other[i % 2, rows].astype(jnp.float32)
                out[i, b, c] = both.astype(jnp.bfloat16)
        if i < 2:
            for copy in load(i + 2):
                copy.start()


def sum_grads(where, grads, theirs):
    columns = grads.shape[1]
    far = pl.BlockSpec(memory_space=pltpu.HBM)
    return pl.pallas_call(
        sum_kernel,
        out_shape=jax.ShapeDtypeStruct((4, 4, 4, 64, columns), jnp.bfloat16),
        in_specs=[pl.BlockSpec(memory_space=pltpu.SMEM), far, far],
        out_specs=pl.BlockSpec(memory_space=pltpu.VMEM),
        scratch_shapes=[
            pltpu.VMEM((2, 1024, columns), jnp.bfloat16),
            pltpu.VMEM((2, 1024, columns), jnp.bfloat16),
            pltpu.SemaphoreType.DMA((2, 2)),
        ],
        compiler_params=pltpu.CompilerParams(vmem_limit_bytes=40 * MIB),
        cost_estimate=pl.CostEstimate(flops=4096 * columns, bytes_accessed=24576 * columns, transcendentals=0),
        name="sum_grads",
    )(where, *[pltpu.with_memory_space_constraint(value, pltpu.HBM) for value in (grads, theirs)])


def project_kernel(late, summed, *refs):
    pieces, refs = refs[:6], refs[6:]
    if late:
        where, before, partial, sent, *refs = refs
    else:
        partial, *refs = refs
    packed, scratch, (sems, pack_sem, out_sem) = refs[:3], refs[3:9], refs[9:]
    loads = [pltpu.make_async_copy(p, v, sems.at[k]) for k, (p, v) in enumerate(zip(pieces, scratch))]
    for load in loads:
        load.start()
    for k, load in enumerate(loads):
        load.wait()
        pltpu.make_async_copy(scratch[k], packed[k // 2].at[k % 2], pack_sem).start()
        low, high, axes = STREAMS[k // 2]
        z, y, x = corner(axes, 2 * late + k % 2)
        rows = summed[z, y, x]
        product = lax.dot_general(
            scratch[k][...].reshape(1024, high - low),
            rows.reshape(1024, rows.shape[-1]),
            (((0,), (0,)), ((), ())),
            preferred_element_type=jnp.float32,
        )
        if k % 2:
            partial[low:high] += product
        elif late:
            partial[low:high] = before[low:high] + product
        else:
            partial[low:high] = product
    if late:
        share = sent.shape[1]
        for far in range(2):
            row = pl.multiple_of((far * 2 + 1 - where[0]) * share, share)
            pltpu.make_async_copy(partial.at[pl.ds(row, share)], sent.at[far], out_sem).start()
        pltpu.make_async_copy(sent, sent, out_sem).wait()
    for out in packed:
        pltpu.make_async_copy(out, out, pack_sem).wait()


def project(summed, pieces, where=None, before=None):
    columns = summed.shape[-1]
    late = before is not None
    anywhere, inside = pl.BlockSpec(memory_space=pl.ANY), pl.BlockSpec(memory_space=pltpu.VMEM)
    result = [jax.ShapeDtypeStruct((1024, columns), jnp.float32)]
    if late:
        result.append(jax.ShapeDtypeStruct((2, 256, columns), jnp.float32))
    packed = [jax.ShapeDtypeStruct((2, *piece.shape), piece.dtype) for piece in pieces[::2]]
    return pl.pallas_call(
        functools.partial(project_kernel, late),
        out_shape=result + packed,
        in_specs=[inside] + [anywhere] * 6 + [pl.BlockSpec(memory_space=pltpu.SMEM), inside] * late,
        out_specs=[inside] + [anywhere] * (len(result) + 2),
        scratch_shapes=[pltpu.VMEM(piece.shape, jnp.bfloat16) for piece in pieces]
        + [pltpu.SemaphoreType.DMA((6,)), pltpu.SemaphoreType.DMA, pltpu.SemaphoreType.DMA],
        compiler_params=pltpu.CompilerParams(vmem_limit_bytes=32 * MIB),
        cost_estimate=pl.CostEstimate(
            flops=summed.size * 1024, bytes_accessed=2 * summed.size + 4 * MIB, transcendentals=0
        ),
        name="project_late" if late else "project",
    )(summed, *pieces, *([where, before] if late else []))


def chip_kernel(where, partial, received, kept, sent):
    core, far = where[0], where[1] // 2
    share = kept.shape[0]

    def total(f):
        return partial[pl.ds(pl.multiple_of((f * 2 + core) * share, share), share)] + received[f]

    sent[...] = total(1 - far).astype(jnp.bfloat16)
    kept[...] = total(far)


def add_cores(where, partial, received):
    columns = partial.shape[1]
    inside = pl.BlockSpec(memory_space=pltpu.VMEM)
    return pl.pallas_call(
        chip_kernel,
        out_shape=(
            jax.ShapeDtypeStruct((256, columns), jnp.float32),
            jax.ShapeDtypeStruct((256, columns), jnp.bfloat16),
        ),
        in_specs=[pl.BlockSpec(memory_space=pltpu.SMEM), inside, inside],
        out_specs=(inside, inside),
        compiler_params=pltpu.CompilerParams(vmem_limit_bytes=16 * MIB),
        name="add_cores",
    )(where, partial, received)


def adam(kept, received, first_moment, second_moment):
    projected = (kept + received.astype(jnp.float32)) * (1.0 / 4)
    new_first = 0.9 * first_moment + 0.1 * projected
    new_second = 0.999 * second_moment + 0.001 * projected * projected
    return new_first, new_second


def direction_kernel(kept, received, first_moment, second_moment, out):
    new_first, new_second = adam(kept[...], received[...], first_moment[...], second_moment[...])
    out[...] = (new_first / first_fix / (jnp.sqrt(new_second / second_fix) + 1e-08)).astype(jnp.bfloat16)


def direct(*operands):
    inside = pl.BlockSpec(memory_space=pltpu.VMEM)
    return pl.pallas_call(
        direction_kernel,
        out_shape=jax.ShapeDtypeStruct(operands[0].shape, jnp.bfloat16),
        in_specs=[inside] * 4,
        out_specs=inside,
        compiler_params=pltpu.CompilerParams(vmem_limit_bytes=16 * MIB),
        name="direction",
    )(*operands)


SLOTS = 3


def update_kernel(where, *refs):
    own, other, quarters, refs = refs[:12], refs[12:18], refs[18:22], refs[22:]
    bases = own, [other[2 * (k // 4) + (k % 4) // 2].at[k % 2] for k in range(12)]
    out, direction, block, result, in_sems, out_sems = refs
    core, z, y, x = where[0], where[1], where[2], where[3]

    def load(t):
        side, a = t // 4, t % 4
        slot = t % SLOTS
        for k, piece in enumerate(bases[side]):
            low, high, axes = STREAMS[k // 4]
            layers, b, c = corner(axes, k % 4)
            if layers.start <= a < layers.stop:
                pltpu.make_async_copy(
                    piece.at[a - layers.start],
                    block.at[slot, pl.ds(b.start, b.stop - b.start), pl.ds(c.start, c.stop - c.start), :, pl.ds(low, high - low)],
                    in_sems.at[slot],
                ).start()

    def drain(turn):
        pltpu.make_async_copy(result.at[turn], result.at[turn], out_sems.at[turn]).wait()

    for t in range(SLOTS):
        load(t)
    far, share = z // 2, quarters[0].shape[0]
    for k, quarter in enumerate(quarters):
        place = (far ^ (k // 2)) * 2 + (core ^ (k % 2))
        direction[pl.ds(pl.multiple_of(place * share, share), share)] = quarter[...]
    for t in range(8):
        side, a = t // 4, t % 4
        of_core = core if side == 0 else 1 - core
        slot, turn = t % SLOTS, t % 2
        pltpu.make_async_copy(block.at[slot], block.at[slot], in_sems.at[slot]).wait()
        if t >= 2:
            drain(turn)
        base = layer(of_core, z, a) * 1024
        parts = 1 if t < 7 else 2
        for b in range(4):
            if b % (4 // parts) == 0:
                size = 1024 // parts
                result[turn, b * 256 : b * 256 + size] = jnp.dot(
                    block[slot, b : b + 4 // parts].reshape(size, block.shape[-1]),
                    direction[...],
                    preferred_element_type=jnp.float32,
                ).astype(jnp.bfloat16)
            if b == 0 and t + SLOTS < 8:
                load(t + SLOTS)
            for c in range(4):
                row = pl.multiple_of(base + (y ^ offset(of_core, b)) * 256 + (x ^ offset(of_core, c)) * 64, 64)
                pltpu.make_async_copy(
                    result.at[turn, pl.ds((b * 4 + c) * 64, 64)], out.at[pl.ds(row, 64)], out_sems.at[turn]
                ).start()
    drain(0)
    drain(1)


def back_project(where, bases, quarters):
    share, columns = quarters[0].shape
    rank = 4 * share
    rows = 2 * 4096
    anywhere, inside = pl.BlockSpec(memory_space=pl.ANY), pl.BlockSpec(memory_space=pltpu.VMEM)
    return pl.pallas_call(
        update_kernel,
        out_shape=jax.ShapeDtypeStruct((rows, columns), jnp.bfloat16),
        in_specs=[pl.BlockSpec(memory_space=pltpu.SMEM)] + [anywhere] * 18 + [inside] * 4,
        out_specs=anywhere,
        scratch_shapes=[
            pltpu.VMEM((rank, columns), jnp.bfloat16),
            pltpu.VMEM((SLOTS, 4, 4, 64, rank), jnp.bfloat16),
            pltpu.VMEM((2, 1024, columns), jnp.bfloat16),
            pltpu.SemaphoreType.DMA((SLOTS,)),
            pltpu.SemaphoreType.DMA((2,)),
        ],
        compiler_params=pltpu.CompilerParams(vmem_limit_bytes=32 * MIB),
        cost_estimate=pl.CostEstimate(
            flops=2 * rows * rank * columns, bytes_accessed=2 * rows * (rank + columns), transcendentals=0
        ),
        name="back_project",
    )(where, *bases, *quarters)


def local(grads, basis, first_moment, second_moment):
    dp, fsdp = lax.axis_index("dp"), lax.axis_index("fsdp")
    far, core = dp // 2, dp % 2
    z, y, x = far * 2 + fsdp // 16, (fsdp // 4) % 4, fsdp % 4
    where = jnp.stack([core, z, y, x]).astype(jnp.int32)

    whole = grads[0]
    columns = whole.shape[1]
    theirs = swap_core(whole)
    held, theirs = together(cube(basis), theirs)
    eighths = [held[..., low:high] for low, high, _ in STREAMS]
    got = [exchange(eighth, axes[0], 1) for eighth, (_, _, axes) in zip(eighths, STREAMS)]
    ahead = [exchange(eighth, axes[1], 1) for eighth, (_, _, axes) in zip(eighths[:2], STREAMS)]
    got = together(*got)
    halves = [join(eighth, other, axes[0]) for eighth, other, (_, _, axes) in zip(eighths, got, STREAMS)]
    behind = [exchange(other, axes[1], 1) for other, (_, _, axes) in zip(got[:2], STREAMS)]
    third = [exchange(half, axes[2], 1) for half, (_, _, axes) in zip(halves, STREAMS)]
    second = [join(first, last, axes[0]) for first, last, (_, _, axes) in zip(ahead, behind, STREAMS)]
    second.append(exchange(halves[2], STREAMS[2][2][1], 1))
    fourth = [exchange(got, axes[2], 1) for got, (_, _, axes) in zip(second, STREAMS)]
    early = [piece for pair in zip(halves, second) for piece in pair]
    late = [piece for pair in zip(third, fourth) for piece in pair]
    summed = sum_grads(where, whole, theirs)
    partial, *packed = project(summed, early)
    partial, sent, *more = project(summed, late, where, partial)

    kept, sent = add_cores(where, partial, swap_core(sent))
    kept, *more = together(kept, *more)
    received = swap_far(sent)
    direction = direct(kept, received, first_moment, second_moment)
    new_first, new_second = adam(kept, received, first_moment, second_moment)

    distant = swap_far(direction)
    near = swap_core(direction)
    own = [piece for k in range(3) for piece in (*early[2 * k : 2 * k + 2], *late[2 * k : 2 * k + 2])]
    other = [swap_core(value) for pair in zip(packed, more) for value in pair]
    update = back_project(where, own + other, (direction, near, distant, swap_core(distant)))
    return (update, new_first, new_second)


def solution(mesh):
    return jax.shard_map(
        local,
        mesh=mesh,
        in_specs=(P("dp", None, "fsdp"), P(("dp", "fsdp"), None), P("dp", "fsdp"), P("dp", "fsdp")),
        out_specs=(P(None, "fsdp"), P("dp", "fsdp"), P("dp", "fsdp")),
        check_vma=False,
    )
```

```python
import functools
import math

import jax
import jax.numpy as jnp
from jax import lax
from jax.experimental import pallas as pl
from jax.experimental.pallas import tpu as pltpu
from jax.sharding import PartitionSpec as P

first_fix = 1.0 - math.exp(1000.0 * math.log(0.9))
second_fix = 1.0 - math.exp(1000.0 * math.log(0.999))

BOTH = ("dp", "fsdp")
ORDER = ((0, 3, 1, 2), (0, 1, 3, 2))
STREAMS = ((0, 384, "yzx"), (384, 768, "zxy"), (768, 1024, "xyz"))
MIB = 1024 * 1024


def linear(c, z, y, x):
    return (((z // 2) * 2 + c) * 2 + z % 2) * 16 + y * 4 + x


def pairs(partner):
    return [
        (linear(c, z, y, x), linear(*partner(c, z, y, x)))
        for c in range(2)
        for z in range(4)
        for y in range(4)
        for x in range(4)
    ]


def exchange(value, axes, step):
    def partner(c, z, y, x):
        t, u = (ORDER[c][1], ORDER[1 - c][1]) if step == 0 else (ORDER[1 - c][1], ORDER[c][1])
        return c, z ^ u if "z" in axes else z, y ^ t if "y" in axes else y, x ^ t if "x" in axes else x

    return lax.ppermute(value, BOTH, pairs(partner))


def swap_core(value):
    return lax.ppermute(value, BOTH, pairs(lambda c, z, y, x: (1 - c, z, y, x)))


def swap_far(value):
    return lax.ppermute(value, BOTH, pairs(lambda c, z, y, x: (c, z ^ 2, y, x)))


def bring_kernel(source, out, sem):
    copy = pltpu.make_async_copy(source, out, sem)
    copy.start()
    copy.wait()


def bring(value):
    return pl.pallas_call(
        bring_kernel,
        out_shape=jax.ShapeDtypeStruct(value.shape, value.dtype),
        in_specs=[pl.BlockSpec(memory_space=pl.ANY)],
        out_specs=pl.BlockSpec(memory_space=pltpu.VMEM),
        scratch_shapes=[pltpu.SemaphoreType.DMA],
        compiler_params=pltpu.CompilerParams(vmem_limit_bytes=4 * MIB),
        name="bring",
    )(value)


def cube(shard):
    x, y, xy, z = together(*[exchange(shard, axes, 0) for axes in ("x", "y", "xy", "z")])
    xz, yz, xyz = exchange(jnp.stack([x, y, xy]), "z", 0)
    return jnp.stack([bring(shard), x, y, xy, z, xz, yz, xyz]).reshape(2, 2, 2, *shard.shape)


def join(first, second, axis):
    return jnp.concatenate([first, second], axis="zyx".index(axis))


def corner(axes, quarter):
    out = []
    for axis in "zyx":
        late = quarter % 2 if axis == axes[1] else quarter // 2
        out.append(slice(0, 4) if axis == axes[0] else slice(2 * late, 2 * late + 2))
    return tuple(out)


def together(*values):
    return lax.optimization_barrier(values)


def offset(of_core, position):
    one = jnp.where(of_core == 0, 3, 1)
    return jnp.where(position == 0, 0, jnp.where(position == 1, one, jnp.where(position == 2, 4 - one, 2)))


def layer(of_core, z, position):
    zz = z ^ offset(1 - of_core, position)
    return ((zz // 2) * 2 + of_core) * 2 + zz % 2


def sum_kernel(where, grads, theirs, out, mine, other, sems):
    core, z, y, x = where[0], where[1], where[2], where[3]

    def load(i):
        rows = pl.ds(pl.multiple_of(layer(core, z, i) * 1024, 1024), 1024)
        return [
            pltpu.make_async_copy(grads.at[rows], mine.at[i % 2], sems.at[0, i % 2]),
            pltpu.make_async_copy(theirs.at[rows], other.at[i % 2], sems.at[1, i % 2]),
        ]

    for i in range(2):
        for copy in load(i):
            copy.start()
    for i in range(4):
        for copy in load(i):
            copy.wait()
        for b in range(4):
            for c in range(4):
                rows = pl.ds(pl.multiple_of((y ^ offset(core, b)) * 256 + (x ^ offset(core, c)) * 64, 64), 64)
                both = mine[i % 2, rows].astype(jnp.float32) + other[i % 2, rows].astype(jnp.float32)
                out[i, b, c] = both.astype(jnp.bfloat16)
        if i < 2:
            for copy in load(i + 2):
                copy.start()


def sum_grads(where, grads, theirs):
    columns = grads.shape[1]
    far = pl.BlockSpec(memory_space=pltpu.HBM)
    return pl.pallas_call(
        sum_kernel,
        out_shape=jax.ShapeDtypeStruct((4, 4, 4, 64, columns), jnp.bfloat16),
        in_specs=[pl.BlockSpec(memory_space=pltpu.SMEM), far, far],
        out_specs=pl.BlockSpec(memory_space=pltpu.VMEM),
        scratch_shapes=[
            pltpu.VMEM((2, 1024, columns), jnp.bfloat16),
            pltpu.VMEM((2, 1024, columns), jnp.bfloat16),
            pltpu.SemaphoreType.DMA((2, 2)),
        ],
        compiler_params=pltpu.CompilerParams(vmem_limit_bytes=40 * MIB),
        cost_estimate=pl.CostEstimate(flops=4096 * columns, bytes_accessed=24576 * columns, transcendentals=0),
        name="sum_grads",
    )(where, *[pltpu.with_memory_space_constraint(value, pltpu.HBM) for value in (grads, theirs)])


def project_kernel(late, summed, *refs):
    pieces, refs = refs[:6], refs[6:]
    if late:
        where, before, partial, sent, *refs = refs
    else:
        partial, *refs = refs
    packed, scratch, (sems, pack_sem) = refs[:3], refs[3:9], refs[9:]
    loads = [pltpu.make_async_copy(p, v, sems.at[k]) for k, (p, v) in enumerate(zip(pieces, scratch))]
    for load in loads:
        load.start()
    for k, load in enumerate(loads):
        load.wait()
        pltpu.make_async_copy(scratch[k], packed[k // 2].at[k % 2], pack_sem).start()
        low, high, axes = STREAMS[k // 2]
        z, y, x = corner(axes, 2 * late + k % 2)
        rows = summed[z, y, x]
        product = lax.dot_general(
            scratch[k][...].reshape(1024, high - low),
            rows.reshape(1024, rows.shape[-1]),
            (((0,), (0,)), ((), ())),
            preferred_element_type=jnp.float32,
        )
        if k % 2:
            partial[low:high] += product
        elif late:
            partial[low:high] = before[low:high] + product
        else:
            partial[low:high] = product
    if late:
        share = sent.shape[1]
        for far in range(2):
            row = pl.multiple_of((far * 2 + 1 - where[0]) * share, share)
            sent[far] = partial[pl.ds(row, share)].astype(sent.dtype)
    for out in packed:
        pltpu.make_async_copy(out, out, pack_sem).wait()


def project(summed, pieces, where=None, before=None):
    columns = summed.shape[-1]
    late = before is not None
    anywhere, inside = pl.BlockSpec(memory_space=pl.ANY), pl.BlockSpec(memory_space=pltpu.VMEM)
    result = [jax.ShapeDtypeStruct((1024, columns), jnp.float32)]
    if late:
        result.append(jax.ShapeDtypeStruct((2, 256, columns), jnp.bfloat16))
    packed = [jax.ShapeDtypeStruct((2, *piece.shape), piece.dtype) for piece in pieces[::2]]
    return pl.pallas_call(
        functools.partial(project_kernel, late),
        out_shape=result + packed,
        in_specs=[inside] + [anywhere] * 6 + [pl.BlockSpec(memory_space=pltpu.SMEM), inside] * late,
        out_specs=[inside] * len(result) + [anywhere] * 3,
        scratch_shapes=[pltpu.VMEM(piece.shape, jnp.bfloat16) for piece in pieces]
        + [pltpu.SemaphoreType.DMA((6,)), pltpu.SemaphoreType.DMA],
        compiler_params=pltpu.CompilerParams(vmem_limit_bytes=32 * MIB),
        cost_estimate=pl.CostEstimate(
            flops=summed.size * 1024, bytes_accessed=2 * summed.size + 4 * MIB, transcendentals=0
        ),
        name="project_late" if late else "project",
    )(summed, *pieces, *([where, before] if late else []))


def chip_kernel(where, partial, received, kept, sent):
    core, far = where[0], where[1] // 2
    share = kept.shape[0]

    def total(f):
        return partial[pl.ds(pl.multiple_of((f * 2 + core) * share, share), share)] + received[f].astype(jnp.float32)

    sent[...] = total(1 - far).astype(jnp.bfloat16)
    kept[...] = total(far)


def add_cores(where, partial, received):
    columns = partial.shape[1]
    inside = pl.BlockSpec(memory_space=pltpu.VMEM)
    return pl.pallas_call(
        chip_kernel,
        out_shape=(
            jax.ShapeDtypeStruct((256, columns), jnp.float32),
            jax.ShapeDtypeStruct((256, columns), jnp.bfloat16),
        ),
        in_specs=[pl.BlockSpec(memory_space=pltpu.SMEM), inside, inside],
        out_specs=(inside, inside),
        compiler_params=pltpu.CompilerParams(vmem_limit_bytes=16 * MIB),
        name="add_cores",
    )(where, partial, received)


def adam(kept, received, first_moment, second_moment):
    projected = (kept + received.astype(jnp.float32)) * (1.0 / 4)
    new_first = 0.9 * first_moment + 0.1 * projected
    new_second = 0.999 * second_moment + 0.001 * projected * projected
    return new_first, new_second


def direction_kernel(kept, received, first_moment, second_moment, out):
    new_first, new_second = adam(kept[...], received[...], first_moment[...], second_moment[...])
    out[...] = (new_first / first_fix / (jnp.sqrt(new_second / second_fix) + 1e-08)).astype(jnp.bfloat16)


def direct(*operands):
    inside = pl.BlockSpec(memory_space=pltpu.VMEM)
    return pl.pallas_call(
        direction_kernel,
        out_shape=jax.ShapeDtypeStruct(operands[0].shape, jnp.bfloat16),
        in_specs=[inside] * 4,
        out_specs=inside,
        compiler_params=pltpu.CompilerParams(vmem_limit_bytes=16 * MIB),
        name="direction",
    )(*operands)


SLOTS = 3


def update_kernel(where, *refs):
    own, other, quarters, refs = refs[:12], refs[12:18], refs[18:22], refs[22:]
    bases = own, [other[2 * (k // 4) + (k % 4) // 2].at[k % 2] for k in range(12)]
    out, direction, block, result, in_sems, out_sems = refs
    core, z, y, x = where[0], where[1], where[2], where[3]

    def load(t):
        side, a = t // 4, t % 4
        slot = t % SLOTS
        for k, piece in enumerate(bases[side]):
            low, high, axes = STREAMS[k // 4]
            layers, b, c = corner(axes, k % 4)
            if layers.start <= a < layers.stop:
                pltpu.make_async_copy(
                    piece.at[a - layers.start],
                    block.at[slot, pl.ds(b.start, b.stop - b.start), pl.ds(c.start, c.stop - c.start), :, pl.ds(low, high - low)],
                    in_sems.at[slot],
                ).start()

    def drain(turn):
        pltpu.make_async_copy(result.at[turn], result.at[turn], out_sems.at[turn]).wait()

    for t in range(SLOTS):
        load(t)
    far, share = z // 2, quarters[0].shape[0]
    for k, quarter in enumerate(quarters):
        place = (far ^ (k // 2)) * 2 + (core ^ (k % 2))
        direction[pl.ds(pl.multiple_of(place * share, share), share)] = quarter[...]
    for t in range(8):
        side, a = t // 4, t % 4
        of_core = core if side == 0 else 1 - core
        slot, turn = t % SLOTS, t % 2
        pltpu.make_async_copy(block.at[slot], block.at[slot], in_sems.at[slot]).wait()
        if t >= 2:
            drain(turn)
        base = layer(of_core, z, a) * 1024
        parts = 1 if t < 7 else 2
        for b in range(4):
            if b % (4 // parts) == 0:
                size = 1024 // parts
                result[turn, b * 256 : b * 256 + size] = jnp.dot(
                    block[slot, b : b + 4 // parts].reshape(size, block.shape[-1]),
                    direction[...],
                    preferred_element_type=jnp.float32,
                ).astype(jnp.bfloat16)
            if b == 0 and t + SLOTS < 8:
                load(t + SLOTS)
            for c in range(4):
                row = pl.multiple_of(base + (y ^ offset(of_core, b)) * 256 + (x ^ offset(of_core, c)) * 64, 64)
                pltpu.make_async_copy(
                    result.at[turn, pl.ds((b * 4 + c) * 64, 64)], out.at[pl.ds(row, 64)], out_sems.at[turn]
                ).start()
    drain(0)
    drain(1)


def back_project(where, bases, quarters):
    share, columns = quarters[0].shape
    rank = 4 * share
    rows = 2 * 4096
    anywhere, inside = pl.BlockSpec(memory_space=pl.ANY), pl.BlockSpec(memory_space=pltpu.VMEM)
    return pl.pallas_call(
        update_kernel,
        out_shape=jax.ShapeDtypeStruct((rows, columns), jnp.bfloat16),
        in_specs=[pl.BlockSpec(memory_space=pltpu.SMEM)] + [anywhere] * 18 + [inside] * 4,
        out_specs=anywhere,
        scratch_shapes=[
            pltpu.VMEM((rank, columns), jnp.bfloat16),
            pltpu.VMEM((SLOTS, 4, 4, 64, rank), jnp.bfloat16),
            pltpu.VMEM((2, 1024, columns), jnp.bfloat16),
            pltpu.SemaphoreType.DMA((SLOTS,)),
            pltpu.SemaphoreType.DMA((2,)),
        ],
        compiler_params=pltpu.CompilerParams(vmem_limit_bytes=32 * MIB),
        cost_estimate=pl.CostEstimate(
            flops=2 * rows * rank * columns, bytes_accessed=2 * rows * (rank + columns), transcendentals=0
        ),
        name="back_project",
    )(where, *bases, *quarters)


def local(grads, basis, first_moment, second_moment):
    dp, fsdp = lax.axis_index("dp"), lax.axis_index("fsdp")
    far, core = dp // 2, dp % 2
    z, y, x = far * 2 + fsdp // 16, (fsdp // 4) % 4, fsdp % 4
    where = jnp.stack([core, z, y, x]).astype(jnp.int32)

    whole = grads[0]
    columns = whole.shape[1]
    theirs = swap_core(whole)
    held, theirs = together(cube(basis), theirs)
    eighths = [held[..., low:high] for low, high, _ in STREAMS]
    got = [exchange(eighth, axes[0], 1) for eighth, (_, _, axes) in zip(eighths, STREAMS)]
    ahead = [exchange(eighth, axes[1], 1) for eighth, (_, _, axes) in zip(eighths[:2], STREAMS)]
    got = together(*got)
    halves = [join(eighth, other, axes[0]) for eighth, other, (_, _, axes) in zip(eighths, got, STREAMS)]
    behind = [exchange(other, axes[1], 1) for other, (_, _, axes) in zip(got[:2], STREAMS)]
    third = [exchange(half, axes[2], 1) for half, (_, _, axes) in zip(halves, STREAMS)]
    second = [join(first, last, axes[0]) for first, last, (_, _, axes) in zip(ahead, behind, STREAMS)]
    second.append(exchange(halves[2], STREAMS[2][2][1], 1))
    fourth = [exchange(got, axes[2], 1) for got, (_, _, axes) in zip(second, STREAMS)]
    early = [piece for pair in zip(halves, second) for piece in pair]
    late = [piece for pair in zip(third, fourth) for piece in pair]
    summed = sum_grads(where, whole, theirs)
    partial, *packed = project(summed, early)
    partial, sent, *more = project(summed, late, where, partial)

    kept, sent = add_cores(where, partial, swap_core(sent))
    received, *more = together(swap_far(sent), *more)
    direction = direct(kept, received, first_moment, second_moment)
    new_first, new_second = adam(kept, received, first_moment, second_moment)

    distant = swap_far(direction)
    near = swap_core(direction)
    own = [piece for k in range(3) for piece in (*early[2 * k : 2 * k + 2], *late[2 * k : 2 * k + 2])]
    other = [swap_core(value) for pair in zip(packed, more) for value in pair]
    update = back_project(where, own + other, (direction, near, distant, swap_core(distant)))
    return (update, new_first, new_second)


def solution(mesh):
    return jax.shard_map(
        local,
        mesh=mesh,
        in_specs=(P("dp", None, "fsdp"), P(("dp", "fsdp"), None), P("dp", "fsdp"), P("dp", "fsdp")),
        out_specs=(P(None, "fsdp"), P("dp", "fsdp"), P("dp", "fsdp")),
        check_vma=False,
    )
```

```python
import functools
import math

import jax
import jax.numpy as jnp
from jax import lax
from jax.experimental import pallas as pl
from jax.experimental.pallas import tpu as pltpu
from jax.sharding import PartitionSpec as P

first_fix = 1.0 - math.exp(1000.0 * math.log(0.9))
second_fix = 1.0 - math.exp(1000.0 * math.log(0.999))

BOTH = ("dp", "fsdp")
ORDER = ((0, 3, 1, 2), (0, 1, 3, 2))
STREAMS = ((0, 384, "yzx"), (384, 768, "zxy"), (768, 1024, "xyz"))
MIB = 1024 * 1024


def linear(c, z, y, x):
    return (((z // 2) * 2 + c) * 2 + z % 2) * 16 + y * 4 + x


def pairs(partner):
    return [
        (linear(c, z, y, x), linear(*partner(c, z, y, x)))
        for c in range(2)
        for z in range(4)
        for y in range(4)
        for x in range(4)
    ]


def exchange(value, axes, step):
    def partner(c, z, y, x):
        t, u = (ORDER[c][1], ORDER[1 - c][1]) if step == 0 else (ORDER[1 - c][1], ORDER[c][1])
        return c, z ^ u if "z" in axes else z, y ^ t if "y" in axes else y, x ^ t if "x" in axes else x

    return lax.ppermute(value, BOTH, pairs(partner))


def swap_core(value):
    return lax.ppermute(value, BOTH, pairs(lambda c, z, y, x: (1 - c, z, y, x)))


def swap_far(value):
    return lax.ppermute(value, BOTH, pairs(lambda c, z, y, x: (c, z ^ 2, y, x)))


def bring_kernel(source, out, sem):
    copy = pltpu.make_async_copy(source, out, sem)
    copy.start()
    copy.wait()


def bring(value):
    return pl.pallas_call(
        bring_kernel,
        out_shape=jax.ShapeDtypeStruct(value.shape, value.dtype),
        in_specs=[pl.BlockSpec(memory_space=pl.ANY)],
        out_specs=pl.BlockSpec(memory_space=pltpu.VMEM),
        scratch_shapes=[pltpu.SemaphoreType.DMA],
        compiler_params=pltpu.CompilerParams(vmem_limit_bytes=4 * MIB),
        name="bring",
    )(value)


def cube(shard):
    x, y, xy, z = together(*[exchange(shard, axes, 0) for axes in ("x", "y", "xy", "z")])
    xz, yz, xyz = exchange(jnp.stack([x, y, xy]), "z", 0)
    return jnp.stack([bring(shard), x, y, xy, z, xz, yz, xyz]).reshape(2, 2, 2, *shard.shape)


def join(first, second, axis):
    return jnp.concatenate([first, second], axis="zyx".index(axis))


def corner(axes, quarter):
    out = []
    for axis in "zyx":
        late = quarter % 2 if axis == axes[1] else quarter // 2
        out.append(slice(0, 4) if axis == axes[0] else slice(2 * late, 2 * late + 2))
    return tuple(out)


def together(*values):
    return lax.optimization_barrier(values)


def offset(of_core, position):
    one = jnp.where(of_core == 0, 3, 1)
    return jnp.where(position == 0, 0, jnp.where(position == 1, one, jnp.where(position == 2, 4 - one, 2)))


def layer(of_core, z, position):
    zz = z ^ offset(1 - of_core, position)
    return ((zz // 2) * 2 + of_core) * 2 + zz % 2


def sum_kernel(where, grads, theirs, out, mine, other, sems):
    core, z, y, x = where[0], where[1], where[2], where[3]

    def load(i):
        rows = pl.ds(pl.multiple_of(layer(core, z, i) * 1024, 1024), 1024)
        return [
            pltpu.make_async_copy(grads.at[rows], mine.at[i % 2], sems.at[0, i % 2]),
            pltpu.make_async_copy(theirs.at[rows], other.at[i % 2], sems.at[1, i % 2]),
        ]

    for i in range(2):
        for copy in load(i):
            copy.start()
    for i in range(4):
        for copy in load(i):
            copy.wait()
        for b in range(4):
            for c in range(4):
                rows = pl.ds(pl.multiple_of((y ^ offset(core, b)) * 256 + (x ^ offset(core, c)) * 64, 64), 64)
                both = mine[i % 2, rows].astype(jnp.float32) + other[i % 2, rows].astype(jnp.float32)
                out[i, b, c] = both.astype(jnp.bfloat16)
        if i < 2:
            for copy in load(i + 2):
                copy.start()


def sum_grads(where, grads, theirs):
    columns = grads.shape[1]
    far = pl.BlockSpec(memory_space=pltpu.HBM)
    return pl.pallas_call(
        sum_kernel,
        out_shape=jax.ShapeDtypeStruct((4, 4, 4, 64, columns), jnp.bfloat16),
        in_specs=[pl.BlockSpec(memory_space=pltpu.SMEM), far, far],
        out_specs=pl.BlockSpec(memory_space=pltpu.VMEM),
        scratch_shapes=[
            pltpu.VMEM((2, 1024, columns), jnp.bfloat16),
            pltpu.VMEM((2, 1024, columns), jnp.bfloat16),
            pltpu.SemaphoreType.DMA((2, 2)),
        ],
        compiler_params=pltpu.CompilerParams(vmem_limit_bytes=40 * MIB),
        cost_estimate=pl.CostEstimate(flops=4096 * columns, bytes_accessed=24576 * columns, transcendentals=0),
        name="sum_grads",
    )(where, *[pltpu.with_memory_space_constraint(value, pltpu.HBM) for value in (grads, theirs)])


def project_kernel(late, summed, *refs):
    pieces, refs = refs[:6], refs[6:]
    if late:
        where, before, partial, sent, *refs = refs
    else:
        partial, *refs = refs
    packed, scratch, (sems, pack_sem) = refs[:3], refs[3:9], refs[9:]
    loads = [pltpu.make_async_copy(p, v, sems.at[k]) for k, (p, v) in enumerate(zip(pieces, scratch))]
    for load in loads:
        load.start()
    for k, load in enumerate(loads):
        load.wait()
        pltpu.make_async_copy(scratch[k], packed[k // 2].at[k % 2], pack_sem).start()
        low, high, axes = STREAMS[k // 2]
        z, y, x = corner(axes, 2 * late + k % 2)
        rows = summed[z, y, x]
        product = lax.dot_general(
            scratch[k][...].reshape(1024, high - low),
            rows.reshape(1024, rows.shape[-1]),
            (((0,), (0,)), ((), ())),
            preferred_element_type=jnp.float32,
        )
        if k % 2:
            partial[low:high] += product
        elif late:
            partial[low:high] = before[low:high] + product
        else:
            partial[low:high] = product
    if late:
        share = sent.shape[1]
        for far in range(2):
            row = pl.multiple_of((far * 2 + 1 - where[0]) * share, share)
            sent[far] = partial[pl.ds(row, share)].astype(sent.dtype)
    for out in packed:
        pltpu.make_async_copy(out, out, pack_sem).wait()


def project(summed, pieces, where=None, before=None):
    columns = summed.shape[-1]
    late = before is not None
    anywhere, inside = pl.BlockSpec(memory_space=pl.ANY), pl.BlockSpec(memory_space=pltpu.VMEM)
    result = [jax.ShapeDtypeStruct((1024, columns), jnp.float32)]
    if late:
        result.append(jax.ShapeDtypeStruct((2, 256, columns), jnp.bfloat16))
    packed = [jax.ShapeDtypeStruct((2, *piece.shape), piece.dtype) for piece in pieces[::2]]
    return pl.pallas_call(
        functools.partial(project_kernel, late),
        out_shape=result + packed,
        in_specs=[inside] + [anywhere] * 6 + [pl.BlockSpec(memory_space=pltpu.SMEM), inside] * late,
        out_specs=[inside] * len(result) + [anywhere] * 3,
        scratch_shapes=[pltpu.VMEM(piece.shape, jnp.bfloat16) for piece in pieces]
        + [pltpu.SemaphoreType.DMA((6,)), pltpu.SemaphoreType.DMA],
        compiler_params=pltpu.CompilerParams(vmem_limit_bytes=32 * MIB),
        cost_estimate=pl.CostEstimate(
            flops=summed.size * 1024, bytes_accessed=2 * summed.size + 4 * MIB, transcendentals=0
        ),
        name="project_late" if late else "project",
    )(summed, *pieces, *([where, before] if late else []))


def chip_kernel(where, partial, received, kept, sent):
    core, far = where[0], where[1] // 2
    share = kept.shape[0]

    def total(f):
        return partial[pl.ds(pl.multiple_of((f * 2 + core) * share, share), share)] + received[f].astype(jnp.float32)

    sent[...] = total(1 - far).astype(jnp.bfloat16)
    kept[...] = total(far)


def add_cores(where, partial, received):
    columns = partial.shape[1]
    inside = pl.BlockSpec(memory_space=pltpu.VMEM)
    return pl.pallas_call(
        chip_kernel,
        out_shape=(
            jax.ShapeDtypeStruct((256, columns), jnp.float32),
            jax.ShapeDtypeStruct((256, columns), jnp.bfloat16),
        ),
        in_specs=[pl.BlockSpec(memory_space=pltpu.SMEM), inside, inside],
        out_specs=(inside, inside),
        compiler_params=pltpu.CompilerParams(vmem_limit_bytes=16 * MIB),
        name="add_cores",
    )(where, partial, received)


def adam(kept, received, first_moment, second_moment):
    projected = (kept + received.astype(jnp.float32)) * (1.0 / 4)
    new_first = 0.9 * first_moment + 0.1 * projected
    new_second = 0.999 * second_moment + 0.001 * projected * projected
    return new_first, new_second


def direction_kernel(kept, received, first_moment, second_moment, out):
    new_first, new_second = adam(kept[...], received[...], first_moment[...], second_moment[...])
    out[...] = (new_first / first_fix / (jnp.sqrt(new_second / second_fix) + 1e-08)).astype(jnp.bfloat16)


def direct(*operands):
    inside = pl.BlockSpec(memory_space=pltpu.VMEM)
    return pl.pallas_call(
        direction_kernel,
        out_shape=jax.ShapeDtypeStruct(operands[0].shape, jnp.bfloat16),
        in_specs=[inside] * 4,
        out_specs=inside,
        compiler_params=pltpu.CompilerParams(vmem_limit_bytes=16 * MIB),
        name="direction",
    )(*operands)


SLOTS = 3


def update_kernel(where, *refs):
    own, other, quarters, refs = refs[:12], refs[12:18], refs[18:22], refs[22:]
    bases = own, [other[2 * (k // 4) + (k % 4) // 2].at[k % 2] for k in range(12)]
    out, direction, block, result, in_sems, out_sems = refs
    core, z, y, x = where[0], where[1], where[2], where[3]

    def load(t):
        side, a = t // 4, t % 4
        slot = t % SLOTS
        for k, piece in enumerate(bases[side]):
            low, high, axes = STREAMS[k // 4]
            layers, b, c = corner(axes, k % 4)
            if layers.start <= a < layers.stop:
                pltpu.make_async_copy(
                    piece.at[a - layers.start],
                    block.at[slot, pl.ds(b.start, b.stop - b.start), pl.ds(c.start, c.stop - c.start), :, pl.ds(low, high - low)],
                    in_sems.at[slot],
                ).start()

    def drain(turn):
        pltpu.make_async_copy(result.at[turn], result.at[turn], out_sems.at[turn]).wait()

    for t in range(SLOTS):
        load(t)
    far, share = z // 2, quarters[0].shape[0]
    for k, quarter in enumerate(quarters):
        place = (far ^ (k // 2)) * 2 + (core ^ (k % 2))
        direction[pl.ds(pl.multiple_of(place * share, share), share)] = quarter[...]
    for t in range(8):
        side, a = t // 4, t % 4
        of_core = core if side == 0 else 1 - core
        slot, turn = t % SLOTS, t % 2
        pltpu.make_async_copy(block.at[slot], block.at[slot], in_sems.at[slot]).wait()
        if t >= 2:
            drain(turn)
        base = layer(of_core, z, a) * 1024
        parts = 1 if t < 7 else 2
        for b in range(4):
            if b % (4 // parts) == 0:
                size = 1024 // parts
                result[turn, b * 256 : b * 256 + size] = jnp.dot(
                    block[slot, b : b + 4 // parts].reshape(size, block.shape[-1]),
                    direction[...],
                    preferred_element_type=jnp.float32,
                ).astype(jnp.bfloat16)
            if b == 0 and t + SLOTS < 8:
                load(t + SLOTS)
            for c in range(4):
                row = pl.multiple_of(base + (y ^ offset(of_core, b)) * 256 + (x ^ offset(of_core, c)) * 64, 64)
                pltpu.make_async_copy(
                    result.at[turn, pl.ds((b * 4 + c) * 64, 64)], out.at[pl.ds(row, 64)], out_sems.at[turn]
                ).start()
    drain(0)
    drain(1)


def back_project(where, bases, quarters):
    share, columns = quarters[0].shape
    rank = 4 * share
    rows = 2 * 4096
    anywhere, inside = pl.BlockSpec(memory_space=pl.ANY), pl.BlockSpec(memory_space=pltpu.VMEM)
    return pl.pallas_call(
        update_kernel,
        out_shape=jax.ShapeDtypeStruct((rows, columns), jnp.bfloat16),
        in_specs=[pl.BlockSpec(memory_space=pltpu.SMEM)] + [anywhere] * 18 + [inside] * 4,
        out_specs=anywhere,
        scratch_shapes=[
            pltpu.VMEM((rank, columns), jnp.bfloat16),
            pltpu.VMEM((SLOTS, 4, 4, 64, rank), jnp.bfloat16),
            pltpu.VMEM((2, 1024, columns), jnp.bfloat16),
            pltpu.SemaphoreType.DMA((SLOTS,)),
            pltpu.SemaphoreType.DMA((2,)),
        ],
        compiler_params=pltpu.CompilerParams(vmem_limit_bytes=32 * MIB),
        cost_estimate=pl.CostEstimate(
            flops=2 * rows * rank * columns, bytes_accessed=2 * rows * (rank + columns), transcendentals=0
        ),
        name="back_project",
    )(where, *bases, *quarters)


def local(grads, basis, first_moment, second_moment):
    dp, fsdp = lax.axis_index("dp"), lax.axis_index("fsdp")
    far, core = dp // 2, dp % 2
    z, y, x = far * 2 + fsdp // 16, (fsdp // 4) % 4, fsdp % 4
    where = jnp.stack([core, z, y, x]).astype(jnp.int32)

    whole = grads[0]
    columns = whole.shape[1]
    theirs = swap_core(whole)
    held, theirs = together(cube(basis), theirs)
    eighths = [held[..., low:high] for low, high, _ in STREAMS]
    got = [exchange(eighth, axes[0], 1) for eighth, (_, _, axes) in zip(eighths, STREAMS)]
    ahead = [exchange(eighth, axes[1], 1) for eighth, (_, _, axes) in zip(eighths[:2], STREAMS)]
    got = together(*got)
    halves = [join(eighth, other, axes[0]) for eighth, other, (_, _, axes) in zip(eighths, got, STREAMS)]
    behind = [exchange(other, axes[1], 1) for other, (_, _, axes) in zip(got[:2], STREAMS)]
    third = [exchange(half, axes[2], 1) for half, (_, _, axes) in zip(halves, STREAMS)]
    second = [join(first, last, axes[0]) for first, last, (_, _, axes) in zip(ahead, behind, STREAMS)]
    second.append(exchange(halves[2], STREAMS[2][2][1], 1))
    fourth = [exchange(got, axes[2], 1) for got, (_, _, axes) in zip(second, STREAMS)]
    early = [piece for pair in zip(halves, second) for piece in pair]
    late = [piece for pair in zip(third, fourth) for piece in pair]
    summed = sum_grads(where, whole, theirs)
    partial, *packed = project(summed, early)
    partial, sent, *more = project(summed, late, where, partial)

    kept, sent = add_cores(where, partial, swap_core(sent))
    received = swap_far(sent)
    direction = direct(kept, received, first_moment, second_moment)
    new_first, new_second = adam(kept, received, first_moment, second_moment)
    new_first, *more = together(new_first, *more)

    distant = swap_far(direction)
    near = swap_core(direction)
    own = [piece for k in range(3) for piece in (*early[2 * k : 2 * k + 2], *late[2 * k : 2 * k + 2])]
    other = [swap_core(value) for pair in zip(packed, more) for value in pair]
    update = back_project(where, own + other, (direction, near, distant, swap_core(distant)))
    return (update, new_first, new_second)


def solution(mesh):
    return jax.shard_map(
        local,
        mesh=mesh,
        in_specs=(P("dp", None, "fsdp"), P(("dp", "fsdp"), None), P("dp", "fsdp"), P("dp", "fsdp")),
        out_specs=(P(None, "fsdp"), P("dp", "fsdp"), P("dp", "fsdp")),
        check_vma=False,
    )
```
